256 devices in a mesh: dp: 8 (over x, core), ctx: 32 (over z, y).
Axes of the slice: x: 4, y: 4, z: 8, core: 2. Of those that a mesh axis runs over, the one named last changes fastest.
Arguments:
- q_proj: bfloat16 [16384, 4096], P('ctx', 'dp'), may hold values from -6 to 6
- k_proj: bfloat16 [16384, 4096], P('ctx', 'dp'), may hold values from -6 to 6
- v_proj: bfloat16 [16384, 4096], P('ctx', 'dp'), may hold values from -6 to 6
- short_taps: float32 [3, 3, 4096], P(None, None, 'dp'), may hold values from -3 to 3
- long_filter: bfloat16 [16384, 4096], P('ctx', 'dp'), may hold values from -0.046875 to 0.046875
- skip_gain: float32 [4096], P('dp'), may hold values from -4 to 4
- w_out: bfloat16 [4096, 4096], P('dp'), may hold values from -0.125 to 0.125
Outputs:
- layer_out: bfloat16 [16384, 4096], P('ctx', 'dp')
The draws below stay inside these ranges and needn't reach their ends.
All inputs are finite; a program needn't handle non-finite values.
Results may differ from the reference program's by a relative error of at most 0.006.
Values may be sent and summed in bfloat16 or wider, within the bound.
A program may use at most 128 MiB of HBM per device.

```python
import jax
import jax.numpy as jnp
from jax import lax

CH = 4096
LEN = 16384


def raised(array, key, source, target, parts, factor):
    owner, partner = [(jnp.arange(array.shape[position]) // (array.shape[position] // parts)).reshape([-1 if axis == position else 1 for axis in range(array.ndim)]) for position in (source, target)]
    chosen = jax.random.permutation(key, parts)[partner]
    strong = (owner == chosen) | (owner == (partner + parts // 2) % parts)
    return jnp.where(strong, factor * array, array)


def level_of(own_key, dims, pieces, low, top_value):
    factor_of = 1.0
    for axis_at, parts in pieces:
        heights = jax.random.uniform(jax.random.fold_in(jax.random.fold_in(own_key, 6), axis_at), (parts,), jnp.float32, low / len(pieces), top_value / len(pieces))
        factor_of = factor_of * jnp.repeat(jnp.exp(heights), dims[axis_at] // parts).reshape((-1,) + (1,) * (len(dims) - 1 - axis_at))
    return factor_of


def normal_values(key, extent, deviation, bound, cuts=(), dtype=jnp.bfloat16):
    array = jax.random.normal(key, extent, jnp.float32) * deviation
    if len(cuts) > 0:
        array = level_of(key, extent, cuts, -0.22, 0.18) * array
    return jnp.clip(array, min=-bound, max=bound).astype(dtype)


def heavy_noise(rng, dims, width, most, cuts, heavy, held_as=jnp.bfloat16):
    array = width * jax.random.normal(rng, dims, jnp.float32)
    if cuts:
        array = array * level_of(rng, dims, cuts, -0.22, 0.18)
    return jnp.clip(raised(array, jax.random.fold_in(rng, 3), *heavy), -most, most).astype(held_as)


def setup_inputs(seed: int = 0) -> dict:
    arg_keys = jax.random.split(jax.random.key(seed), 8)
    q_proj = normal_values(arg_keys[0], (LEN, CH), 1.0, 6.0, ((0, 32), (1, 8)))
    k_proj = normal_values(arg_keys[1], (LEN, CH), 1.0, 6.0, ((0, 32), (1, 8)))
    v_proj = normal_values(arg_keys[2], (LEN, CH), 1.0, 6.0, ((0, 32), (1, 8)))
    short_taps = normal_values(arg_keys[3], (3, 3, CH), 0.5, 3.0, ((2, 8),), jnp.float32)
    long_filter = normal_values(arg_keys[4], (LEN, CH), LEN ** -0.5, 0.046875, ((0, 32), (1, 8)))
    skip_gain = normal_values(arg_keys[5], (CH,), 1.0, 4.0, ((0, 8),), jnp.float32)
    w_out = heavy_noise(arg_keys[6], (CH, CH), CH ** -0.5, 0.125, ((0, 8),), (0, 1, 8, 2.0))
    return {"q_proj": q_proj, "k_proj": k_proj, "v_proj": v_proj, "short_taps": short_taps, "long_filter": long_filter, "skip_gain": skip_gain, "w_out": w_out}


def short_filter(sequence, filter_taps):
    padded = jnp.pad(sequence.astype(jnp.float32), ((2, 0), (0, 0)))
    return filter_taps[0] * padded[2:] + filter_taps[1] * padded[1:-1] + filter_taps[2] * padded[:-2]


def causal_block(pair):
    signal, kernel = pair
    spectrum = jnp.fft.rfft(signal, n=2 * LEN, axis=0) * jnp.fft.rfft(kernel, n=2 * LEN, axis=0)
    return jnp.fft.irfft(spectrum, n=2 * LEN, axis=0)[:LEN]


def reference(q_proj, k_proj, v_proj, short_taps, long_filter, skip_gain, w_out):
    queries = short_filter(q_proj, short_taps[0])
    key_side = short_filter(k_proj, short_taps[1])
    value_side = short_filter(v_proj, short_taps[2])
    mixed_in = (key_side * value_side).astype(jnp.bfloat16)
    block_width = min(CH, 256)
    block_count = CH // block_width
    signal = mixed_in.astype(jnp.float32).reshape(LEN, block_count, block_width).transpose(1, 0, 2)
    kernel = long_filter.astype(jnp.float32).reshape(LEN, block_count, block_width).transpose(1, 0, 2)
    convolved = lax.map(causal_block, (signal, kernel))
    convolved = convolved.transpose(1, 0, 2).reshape(LEN, CH).astype(jnp.bfloat16)
    gated = (queries * (convolved.astype(jnp.float32) + skip_gain * mixed_in.astype(jnp.float32))).astype(jnp.bfloat16)
    return jnp.dot(gated, w_out, preferred_element_type=jnp.float32).astype(jnp.bfloat16)
```

```python
import functools
import math

import jax
import jax.numpy as jnp
import ml_dtypes
import numpy as np
from jax import lax
from jax.experimental import pallas as pl
from jax.experimental.pallas import tpu as pltpu
from jax.sharding import PartitionSpec as P

BF16 = jnp.bfloat16
F32 = jnp.float32


def halves(table):
    high = table.astype(ml_dtypes.bfloat16)
    low = (table - high.astype(np.float64)).astype(ml_dtypes.bfloat16)
    return high, low


@functools.lru_cache(None)
def tables(side):
    total = side * side
    index = np.arange(side)
    quarter = index + 0.25
    outer = -2.0 * math.pi * quarter[:, None] * index[None, :] / side
    high, low = halves(np.concatenate([np.cos(outer), np.sin(outer)], axis=0))
    first = np.concatenate([high, low], axis=1)
    turn = -2.0 * math.pi * quarter[:, None] * index[None, :] / total
    twist = np.stack([np.cos(turn), np.sin(turn)]).astype(np.float32)
    inner = -2.0 * math.pi * index[:, None] * index[None, :] / side
    cosine, sine = np.cos(inner), np.sin(inner)
    high, low = halves(np.block([[cosine, sine], [-sine, cosine]]))
    second = np.concatenate([high, high, low], axis=0)
    high, low = halves(np.block([[cosine, -sine], [sine, cosine]]))
    second_back = np.concatenate([high, high, low], axis=0)
    high, low = halves(np.concatenate([np.cos(outer).T, np.sin(outer).T], axis=1) / total)
    first_back = np.concatenate([high, high, low], axis=1)
    return first, twist, second, second_back, first_back


def split(value):
    high = value.astype(BF16)
    low = (value - high.astype(F32)).astype(BF16)
    return high, low


def conv_kernel(x_ref, h_ref, first_ref, twist_ref, second_ref, second_back_ref, first_back_ref, y_ref):
    channels, side, _ = x_ref.shape
    group = 2

    def spectrum(ref, base):
        data = jnp.concatenate([ref[base + i] for i in range(group)], axis=1)
        part = jnp.dot(
            first_ref[...], jnp.concatenate([data, data], axis=0), preferred_element_type=F32
        )
        rows = []
        for i in range(group):
            lanes = slice(i * side, (i + 1) * side)
            real, imag = part[:side, lanes], part[side:, lanes]
            rows.append(
                jnp.concatenate(
                    [
                        real * twist_ref[0] - imag * twist_ref[1],
                        real * twist_ref[1] + imag * twist_ref[0],
                    ],
                    axis=1,
                )
            )
        high, low = split(jnp.concatenate(rows, axis=0))
        return jnp.dot(
            jnp.concatenate([high, low, high], axis=1), second_ref[...], preferred_element_type=F32
        )

    @pl.loop(0, channels // group)
    def _(step):
        base = step * group
        x_spec = spectrum(x_ref, base)
        h_spec = spectrum(h_ref, base)
        x_real, x_imag = x_spec[:, :side], x_spec[:, side:]
        h_real, h_imag = h_spec[:, :side], h_spec[:, side:]
        product = jnp.concatenate(
            [x_real * h_real - x_imag * h_imag, x_real * h_imag + x_imag * h_real], axis=1
        )
        high, low = split(product)
        back = jnp.dot(
            jnp.concatenate([high, low, high], axis=1),
            second_back_ref[...],
            preferred_element_type=F32,
        )
        columns = []
        for i in range(group):
            rows = slice(i * side, (i + 1) * side)
            real, imag = back[rows, :side], back[rows, side:]
            high, low = split(
                jnp.concatenate(
                    [
                        real * twist_ref[0] + imag * twist_ref[1],
                        imag * twist_ref[0] - real * twist_ref[1],
                    ],
                    axis=0,
                )
            )
            columns.append(jnp.concatenate([high, low, high], axis=0))
        values = jnp.dot(
            first_back_ref[...], jnp.concatenate(columns, axis=1), preferred_element_type=F32
        ).astype(BF16)
        for i in range(group):
            y_ref[base + i] = values[:, i * side : (i + 1) * side]


def long_conv(x, h):
    side = x.shape[1]
    return pl.pallas_call(
        conv_kernel,
        out_shape=jax.ShapeDtypeStruct(x.shape, BF16),
        in_specs=[pl.BlockSpec(memory_space=pltpu.VMEM)] * 7,
        out_specs=pl.BlockSpec(memory_space=pltpu.VMEM),
        compiler_params=pltpu.CompilerParams(vmem_limit_bytes=32 * 1024 * 1024),
    )(x, h, *[jnp.asarray(t) for t in tables(side)])


def from_behind(block, axis, distance):
    devices = range(lax.axis_size(axis))
    route = [(i - distance, i) for i in devices if i - distance in devices]
    return lax.ppermute(block, axis, route)


def short_filter(current, previous, filter_taps):
    extended = jnp.concatenate([previous, current], axis=0).astype(F32)
    return (
        filter_taps[0] * extended[2:]
        + filter_taps[1] * extended[1:-1]
        + filter_taps[2] * extended[:-2]
    )


def body(q_proj, k_proj, v_proj, short_taps, long_filter, skip_gain, w_out):
    parts = lax.axis_size("ctx")
    rows, channels = q_proj.shape
    mine = channels // parts
    side = math.isqrt(rows * parts)
    rim_rows = jnp.stack([q_proj[-2:], k_proj[-2:], v_proj[-2:]])
    previous = from_behind(rim_rows, "ctx", 1)
    queries = short_filter(q_proj, previous[0], short_taps[0])
    key_side = short_filter(k_proj, previous[1], short_taps[1])
    value_side = short_filter(v_proj, previous[2], short_taps[2])
    mixed_in = (key_side * value_side).astype(BF16)

    both = jnp.stack([mixed_in.T, long_filter.T]).reshape(2, parts, mine, rows)
    both = both.transpose(1, 0, 2, 3)
    both = lax.all_to_all(both, "ctx", split_axis=0, concat_axis=0, tiled=True)
    both = both.transpose(1, 2, 0, 3).reshape(2, mine, side, side)
    values = long_conv(both[0], both[1])
    values = values.reshape(mine, parts, rows).transpose(1, 0, 2)
    values = lax.all_to_all(values, "ctx", split_axis=0, concat_axis=0, tiled=True)
    convolved = values.reshape(channels, rows).T
    gated = (
        queries * (convolved.astype(F32) + skip_gain * mixed_in.astype(F32))
    ).astype(BF16)
    summed = lax.psum_scatter(
        lax.dot_general(w_out, gated, (((0,), (1,)), ((), ())), preferred_element_type=F32),
        "dp",
        scatter_dimension=0,
        tiled=True,
    )
    return summed.T.astype(BF16)


def solution(mesh):
    placed = (
        P("ctx", "dp"),
        P("ctx", "dp"),
        P("ctx", "dp"),
        P(None, None, "dp"),
        P("ctx", "dp"),
        P("dp"),
        P("dp", None),
    )
    return jax.shard_map(
        body, mesh=mesh, in_specs=placed, out_specs=P("ctx", "dp"), check_vma=False
    )
```

```python
import functools
import math

import jax
import jax.numpy as jnp
import ml_dtypes
import numpy as np
from jax import lax
from jax.experimental import pallas as pl
from jax.experimental.pallas import tpu as pltpu
from jax.sharding import PartitionSpec as P

BF16 = jnp.bfloat16
F32 = jnp.float32
MESH = pl.DeviceIdType.MESH

ROWS = 512
CHANNELS = 512
PARTS = 32
CHIPS = 4
SIDE = 128
CUTS = ROWS // SIDE
CHUNK = 8
COLUMNS = 512
HALF = ROWS // 2
STRIP = COLUMNS // 2


def halves(table):
    high = table.astype(ml_dtypes.bfloat16)
    low = (table - high.astype(np.float64)).astype(ml_dtypes.bfloat16)
    return high, low


@functools.lru_cache(None)
def tables(side):
    total = side * side
    index = np.arange(side)
    quarter = index + 0.25
    outer = -2.0 * math.pi * quarter[:, None] * index[None, :] / side
    high, low = halves(np.concatenate([np.cos(outer), np.sin(outer)], axis=0))
    first = np.concatenate([high, low], axis=1)
    turn = -2.0 * math.pi * quarter[:, None] * index[None, :] / total
    twist = np.stack([np.cos(turn), np.sin(turn)]).astype(np.float32)
    inner = -2.0 * math.pi * index[:, None] * index[None, :] / side
    cosine, sine = np.cos(inner), np.sin(inner)
    high, low = halves(np.block([[cosine, sine], [-sine, cosine]]))
    second = np.concatenate([high, high, low], axis=0)
    high, low = halves(np.block([[cosine, -sine], [sine, cosine]]))
    second_back = np.concatenate([high, high, low], axis=0)
    high, low = halves(np.concatenate([np.cos(outer).T, np.sin(outer).T], axis=1) / total)
    first_back = np.concatenate([high, high, low], axis=1)
    return first, twist, second, second_back, first_back


def split(value):
    high = value.astype(BF16)
    low = (value - high.astype(F32)).astype(BF16)
    return high, low


def kernel(
    q_hbm, k_hbm, v_hbm, h_hbm, w_hbm, taps_ref, skip_ref,
    first_hbm, twist_hbm, second_hbm, second_back_hbm, first_back_hbm,
    out_ref,
    q_in, k_in, v_in, h_in, w_all, first, twist, second, second_back, first_back,
    rim, wide_k, wide_v, turned, mixed, queries,
    h_send, h_recv, x_send, x_recv, flat, spectra, y_flat, y_send, y_recv, back,
    gated, far_send, far_recv, near_send, near_recv,
    load_sem, rim_sems, w_load_sem, w_sems, h_sems, x_sems, y_sems, gated_sems, far_sems, near_sems,
):
    me_dp, me = lax.axis_index("dp"), lax.axis_index("ctx")
    chip, core = me_dp // 2, me_dp % 2
    pair = (chip * 2 + 1 - core, me)
    right = (lax.rem(chip + 1, CHIPS) * 2 + core, me)
    left = (lax.rem(chip + CHIPS - 1, CHIPS) * 2 + core, me)

    def partner(step):
        away = jnp.where(step % 2 == 0, step // 2 + 1, PARTS - (step + 1) // 2)
        return lax.rem(me + away, PARTS)

    barrier = pltpu.get_barrier_semaphore()

    @pl.loop(0, PARTS - 1)
    def _(step):
        pl.semaphore_signal(barrier, inc=1, device_id=(me_dp, partner(step)), device_id_type=MESH)

    for other in (pair, right, left):
        pl.semaphore_signal(barrier, inc=1, device_id=other, device_id_type=MESH)

    loads = [
        pltpu.make_async_copy(source, target, load_sem.at[n])
        for n, (source, target) in enumerate(
            [
                (h_hbm, h_in), (k_hbm, k_in), (v_hbm, v_in), (q_hbm, q_in),
                (first_hbm, first), (twist_hbm, twist), (second_hbm, second),
                (second_back_hbm, second_back), (first_back_hbm, first_back),
            ]
        )
    ]
    for load in loads:
        load.start()

    def remote(source, target, sems, n, device):
        return pltpu.make_async_remote_copy(
            src_ref=source, dst_ref=target, send_sem=sems.at[(0, *n)], recv_sem=sems.at[(1, *n)],
            device_id=device, device_id_type=MESH,
        )

    loads[0].wait()

    @pl.loop(0, CUTS)
    def _(cut):
        rows = pl.ds(pl.multiple_of(cut * SIDE, SIDE), SIDE)
        for tile in range(CHANNELS // SIDE):
            lanes = slice(tile * SIDE, (tile + 1) * SIDE)
            turned[cut, lanes, :] = h_in[rows, lanes].astype(F32).T

    pl.semaphore_wait(barrier, PARTS - 1 + 3)

    rims = [
        remote(hbm.at[pl.ds(ROWS - 16, 16)], rim.at[n], rim_sems, (n,), (me_dp, lax.rem(me + 1, PARTS)))
        for n, hbm in enumerate([q_hbm, k_hbm, v_hbm])
    ]
    for copy in rims:
        copy.start()

    def packed(device, chunk):
        rows = pl.ds(pl.multiple_of(device * 2 * CHUNK + chunk * CHUNK, CHUNK), CHUNK)
        return jnp.concatenate([turned[cut, rows, :] for cut in range(CUTS)], axis=0).astype(BF16)

    @pl.loop(0, PARTS - 1)
    def _(step):
        to = partner(step)
        for chunk in range(2):
            h_send[chunk, to] = packed(to, chunk)
        remote(h_send.at[:, to], h_recv.at[:, me], h_sems, (), (me_dp, to)).start()

    for chunk in range(2):
        h_recv[chunk, me] = packed(me, chunk)

    def widen(source, target, stream):
        target[0:8, :] = jnp.where(me > 0, rim[stream].astype(F32)[8:16, :], 0.0)
        target[8 : 8 + ROWS, :] = source[...].astype(F32)

    def short(wide, stream, cut, lanes):
        window = wide[pl.ds(pl.multiple_of(cut * SIDE, SIDE), SIDE + 8), lanes]
        return (
            taps_ref[stream, 0:1, lanes] * window[8:]
            + taps_ref[stream, 1:2, lanes] * window[7:-1]
            + taps_ref[stream, 2:3, lanes] * window[6:-2]
        )

    loads[1].wait()
    loads[2].wait()
    rims[1].wait()
    rims[2].wait()
    widen(k_in, wide_k, 1)
    widen(v_in, wide_v, 2)

    @pl.loop(0, CUTS)
    def _(cut):
        rows = pl.ds(pl.multiple_of(cut * SIDE, SIDE), SIDE)
        for tile in range(CHANNELS // SIDE):
            lanes = slice(tile * SIDE, (tile + 1) * SIDE)
            value = (short(wide_k, 1, cut, lanes) * short(wide_v, 2, cut, lanes)).astype(BF16)
            mixed[rows, lanes] = value
            turned[cut, lanes, :] = value.astype(F32).T

    for chunk in range(2):

        @pl.loop(0, PARTS - 1)
        def _(step, chunk=chunk):
            to = partner(step)
            x_send[chunk, to] = packed(to, chunk)
            remote(x_send.at[chunk, to], x_recv.at[chunk, me], x_sems, (chunk,), (me_dp, to)).start()

        x_recv[chunk, me] = packed(me, chunk)

    def columns(chip_to, core_to):
        return pl.ds(pl.multiple_of((chip_to * 2 + core_to) * COLUMNS, COLUMNS), COLUMNS)

    w_loads = [
        pltpu.make_async_copy(w_hbm.at[:, columns(n, core)], w_all.at[core, n], w_load_sem.at[n])
        for n in range(CHIPS)
    ]
    w_sent = [
        remote(w_hbm.at[:, columns(n, 1 - core)], w_all.at[core, n], w_sems, (n,), pair)
        for n in range(CHIPS)
    ]
    for copy in w_loads + w_sent:
        copy.start()

    loads[3].wait()
    rims[0].wait()
    widen(q_in, wide_k, 0)

    @pl.loop(0, CUTS)
    def _(cut):
        rows = pl.ds(pl.multiple_of(cut * SIDE, SIDE), SIDE)
        for tile in range(CHANNELS // SIDE):
            lanes = slice(tile * SIDE, (tile + 1) * SIDE)
            queries[rows, lanes] = short(wide_k, 0, cut, lanes)

    def spectrum(base):
        data = jnp.concatenate(
            [flat[pl.ds(base + n, SIDE, stride=CHUNK), :] for n in range(2)], axis=1
        ).astype(BF16)
        part = jnp.dot(first[...], jnp.concatenate([data, data], axis=0), preferred_element_type=F32)
        rows = []
        for n in range(2):
            lanes = slice(n * SIDE, (n + 1) * SIDE)
            real, imag = part[:SIDE, lanes], part[SIDE:, lanes]
            rows.append(
                jnp.concatenate(
                    [real * twist[0] - imag * twist[1], real * twist[1] + imag * twist[0]], axis=1
                )
            )
        high, low = split(jnp.concatenate(rows, axis=0))
        return jnp.dot(
            jnp.concatenate([high, low, high], axis=1), second[...], preferred_element_type=F32
        )

    def all_but_one(send, recv, sems, n=()):
        return remote(send, recv, sems, n, (me_dp, lax.rem(me + 1, PARTS)))

    for load in loads[4:]:
        load.wait()
    some = pl.ds(0, PARTS - 1)
    h_all = all_but_one(h_send.at[:, some], h_recv.at[:, some], h_sems)
    h_all.wait_recv()
    for chunk in range(2):

        @pl.loop(0, PARTS)
        def _(source, chunk=chunk):
            rows = pl.ds(pl.multiple_of(source * CUTS * CHUNK, CUTS * CHUNK), CUTS * CHUNK)
            flat[rows, :] = h_recv[chunk, source].astype(F32)

        @pl.loop(0, CHUNK // 2)
        def _(step, chunk=chunk):
            spectra[chunk * (CHUNK // 2) + step] = spectrum(step * 2)

    sent = []
    for chunk in range(2):
        x_all = all_but_one(x_send.at[chunk, some], x_recv.at[chunk, some], x_sems, (chunk,))
        x_all.wait_recv()
        sent.append(x_all)

        @pl.loop(0, PARTS)
        def _(source, chunk=chunk):
            rows = pl.ds(pl.multiple_of(source * CUTS * CHUNK, CUTS * CHUNK), CUTS * CHUNK)
            flat[rows, :] = x_recv[chunk, source].astype(F32)

        @pl.loop(0, CHUNK // 2)
        def _(step, chunk=chunk):
            x_spec = spectrum(step * 2)
            h_spec = spectra[chunk * (CHUNK // 2) + step]
            x_real, x_imag = x_spec[:, :SIDE], x_spec[:, SIDE:]
            h_real, h_imag = h_spec[:, :SIDE], h_spec[:, SIDE:]
            high, low = split(
                jnp.concatenate(
                    [x_real * h_real - x_imag * h_imag, x_real * h_imag + x_imag * h_real], axis=1
                )
            )
            product = jnp.dot(
                jnp.concatenate([high, low, high], axis=1),
                second_back[...],
                preferred_element_type=F32,
            )
            stacked = []
            for n in range(2):
                rows = slice(n * SIDE, (n + 1) * SIDE)
                real, imag = product[rows, :SIDE], product[rows, SIDE:]
                high, low = split(
                    jnp.concatenate(
                        [real * twist[0] + imag * twist[1], imag * twist[0] - real * twist[1]], axis=0
                    )
                )
                stacked.append(jnp.concatenate([high, low, high], axis=0))
            values = jnp.dot(
                first_back[...], jnp.concatenate(stacked, axis=1), preferred_element_type=F32
            )
            for n in range(2):
                y_flat[pl.ds(step * 2 + n, SIDE, stride=CHUNK), :] = values[:, n * SIDE : (n + 1) * SIDE]

        for half in range(2):

            def piece(device, half=half):
                rows = pl.ds(pl.multiple_of(device * CUTS * CHUNK + half * 16, 16), 16)
                return y_flat[rows, :].astype(BF16)

            @pl.loop(0, PARTS - 1)
            def _(step, chunk=chunk, half=half, piece=piece):
                to = partner(step)
                y_send[chunk, half, to] = piece(to)
                remote(
                    y_send.at[chunk, half, to], y_recv.at[chunk, half, me], y_sems, (chunk, half),
                    (me_dp, to),
                ).start()

            y_recv[chunk, half, me] = piece(me)

    def gate(half):
        for chunk in range(2):
            y_all = all_but_one(
                y_send.at[chunk, half, some], y_recv.at[chunk, half, some], y_sems, (chunk, half)
            )
            y_all.wait_recv()
            sent.append(y_all)

        @pl.loop(0, PARTS)
        def _(source):
            for chunk in range(2):
                value = y_recv[chunk, half, source].astype(F32)
                rows = pl.ds(pl.multiple_of(source * 2 * CHUNK + chunk * CHUNK, CHUNK), CHUNK)
                for n in range(2):
                    back[n, rows, :] = value[n * CHUNK : (n + 1) * CHUNK, :]

        @pl.loop(0, 2)
        def _(n):
            rows = pl.ds(pl.multiple_of(half * HALF + n * SIDE, SIDE), SIDE)
            for tile in range(CHANNELS // SIDE):
                lanes = slice(tile * SIDE, (tile + 1) * SIDE)
                convolved = back[n, lanes, :].T
                direct = skip_ref[0:1, lanes] * mixed[rows, lanes].astype(F32)
                gated[core, rows, lanes] = (queries[rows, lanes] * (convolved + direct)).astype(BF16)

        block = gated.at[core, pl.ds(half * HALF, HALF)]
        copy = remote(block, block, gated_sems, (half,), pair)
        copy.start()
        return copy

    def partial(half, to, strip):
        rows, lanes = slice(half * HALF, (half + 1) * HALF), slice(strip * STRIP, (strip + 1) * STRIP)
        return jnp.dot(
            gated[0, rows, :], w_all[0, to, :, lanes], preferred_element_type=F32
        ) + jnp.dot(gated[1, rows, :], w_all[1, to, :, lanes], preferred_element_type=F32)

    chip_right, chip_left = lax.rem(chip + 1, CHIPS), lax.rem(chip + CHIPS - 1, CHIPS)
    chip_across = lax.rem(chip + 2, CHIPS)
    far, near = {}, {}
    ways = ((0, right, chip_right), (1, left, chip_left))
    for half in range(2):
        exchanged = gate(half)
        if half == 0:
            for copy in w_loads + w_sent:
                copy.wait()
        exchanged.wait()
        for way, device, _ in ways:
            far_send[half, way] = partial(half, chip_across, way).astype(BF16)
            far[half, way] = remote(
                far_send.at[half, way], far_recv.at[half, way], far_sems, (half, way), device
            )
            far[half, way].start()
    for half in range(2):
        for way, device, to in ways:
            far[half, way].wait_recv()
            for strip in range(2):
                value = partial(half, to, strip)
                if strip == way:
                    value = value + far_recv[half, way].astype(F32)
                near_send[half, way, :, strip * STRIP : (strip + 1) * STRIP] = value.astype(BF16)
            near[half, way] = remote(
                near_send.at[half, way], near_recv.at[half, way], near_sems, (half, way), device
            )
            near[half, way].start()
    for half in range(2):
        for way in range(2):
            near[half, way].wait_recv()
        rows = slice(half * HALF, (half + 1) * HALF)
        for strip in range(2):
            lanes = slice(strip * STRIP, (strip + 1) * STRIP)
            out_ref[rows, lanes] = (
                partial(half, chip, strip)
                + near_recv[half, 0, :, lanes].astype(F32)
                + near_recv[half, 1, :, lanes].astype(F32)
            ).astype(BF16)

    for copy in [h_all, *sent, *far.values(), *near.values()]:
        copy.wait_send()


def body(q_proj, k_proj, v_proj, short_taps, long_filter, skip_gain, w_out):
    constants = [jnp.asarray(t) for t in tables(SIDE)]
    wide = (8 + ROWS, CHANNELS)
    stream = (ROWS, CHANNELS)
    travel = (2, PARTS, CUTS * CHUNK, SIDE)
    pieces = (2, 2, PARTS, 16, SIDE)
    dma = pltpu.SemaphoreType.DMA
    anywhere = pl.BlockSpec(memory_space=pl.ANY)
    local = pl.BlockSpec(memory_space=pltpu.VMEM)
    return pl.pallas_call(
        kernel,
        out_shape=jax.ShapeDtypeStruct((ROWS, COLUMNS), BF16),
        in_specs=[anywhere] * 5 + [local] * 2 + [anywhere] * 5,
        out_specs=local,
        scratch_shapes=[
            *[pltpu.VMEM(stream, BF16)] * 4,
            pltpu.VMEM((2, CHIPS, CHANNELS, COLUMNS), BF16),
            *[pltpu.VMEM(t.shape, t.dtype) for t in constants],
            pltpu.VMEM((3, 16, CHANNELS), BF16),
            pltpu.VMEM(wide, F32),
            pltpu.VMEM(wide, F32),
            pltpu.VMEM((CUTS, CHANNELS, SIDE), F32),
            pltpu.VMEM(stream, BF16),
            pltpu.VMEM(stream, F32),
            *[pltpu.VMEM(travel, BF16)] * 4,
            pltpu.VMEM((SIDE * CHUNK, SIDE), F32),
            pltpu.VMEM((CHUNK, 2 * SIDE, 2 * SIDE), F32),
            pltpu.VMEM((SIDE * CHUNK, SIDE), F32),
            *[pltpu.VMEM(pieces, BF16)] * 2,
            pltpu.VMEM((2, CHANNELS, SIDE), F32),
            pltpu.VMEM((2, ROWS, CHANNELS), BF16),
            *[pltpu.VMEM((2, 2, HALF, STRIP), BF16)] * 2,
            *[pltpu.VMEM((2, 2, HALF, COLUMNS), BF16)] * 2,
            dma((9,)),
            dma((2, 3)),
            dma((CHIPS,)),
            dma((2, CHIPS)),
            dma((2,)),
            dma((2, 2)),
            dma((2, 2, 2)),
            dma((2, 2)),
            dma((2, 2, 2)),
            dma((2, 2, 2)),
        ],
        compiler_params=pltpu.CompilerParams(
            collective_id=0, has_side_effects=True, vmem_limit_bytes=56 * 1024 * 1024
        ),
    )(
        q_proj, k_proj, v_proj, long_filter, w_out, short_taps, skip_gain[None, :], *constants
    )


def solution(mesh):
    placed = (
        P("ctx", "dp"),
        P("ctx", "dp"),
        P("ctx", "dp"),
        P(None, None, "dp"),
        P("ctx", "dp"),
        P("dp"),
        P("dp", None),
    )
    return jax.shard_map(
        body, mesh=mesh, in_specs=placed, out_specs=P("ctx", "dp"), check_vma=False
    )
```

```python
import functools
import math

import jax
import jax.numpy as jnp
import ml_dtypes
import numpy as np
from jax import lax
from jax.experimental import pallas as pl
from jax.experimental.pallas import tpu as pltpu
from jax.sharding import PartitionSpec as P

BF16 = jnp.bfloat16
F32 = jnp.float32
MESH = pl.DeviceIdType.MESH

ROWS = 512
CHANNELS = 512
PARTS = 32
CHIPS = 4
SIDE = 128
CUTS = ROWS // SIDE
CHUNK = 8
COLUMNS = 512
HALF = ROWS // 2
STRIP = COLUMNS // 2


def halves(table):
    high = table.astype(ml_dtypes.bfloat16)
    low = (table - high.astype(np.float64)).astype(ml_dtypes.bfloat16)
    return high, low


@functools.lru_cache(None)
def tables(side):
    total = side * side
    index = np.arange(side)
    quarter = index + 0.25
    outer = -2.0 * math.pi * quarter[:, None] * index[None, :] / side
    high, low = halves(np.concatenate([np.cos(outer), np.sin(outer)], axis=0))
    first = np.concatenate([high, low], axis=1)
    turn = -2.0 * math.pi * quarter[:, None] * index[None, :] / total
    twist = np.stack([np.cos(turn), np.sin(turn)]).astype(np.float32)
    inner = -2.0 * math.pi * index[:, None] * index[None, :] / side
    cosine, sine = np.cos(inner), np.sin(inner)
    high, low = halves(np.block([[cosine, sine], [-sine, cosine]]))
    second = np.concatenate([high, high, low], axis=0)
    high, low = halves(np.block([[cosine, -sine], [sine, cosine]]))
    second_back = np.concatenate([high, high, low], axis=0)
    high, low = halves(np.concatenate([np.cos(outer).T, np.sin(outer).T], axis=1) / total)
    first_back = np.concatenate([high, high, low], axis=1)
    return first, twist, second, second_back, first_back


def split(value):
    high = value.astype(BF16)
    low = (value - high.astype(F32)).astype(BF16)
    return high, low


def kernel(
    q_hbm, k_hbm, v_hbm, h_hbm, w_hbm, taps_ref, skip_ref,
    first_hbm, twist_hbm, second_hbm, second_back_hbm, first_back_hbm,
    out_ref,
    q_in, k_in, v_in, h_in, w_all, first, twist, second, second_back, first_back,
    rim, wide_k, wide_v, turned_h, turned_x, mixed, queries,
    h_send, h_recv, x_send, x_recv, flat, spectra, y_flat, y_send, y_recv, back,
    gated, far_send, far_recv, near_send, near_recv,
    load_sem, rim_sems, w_load_sem, w_sems, h_sems, x_sems, y_sems, gated_sems, far_sems, near_sems,
):
    me_dp, me = lax.axis_index("dp"), lax.axis_index("ctx")
    chip, core = me_dp // 2, me_dp % 2
    pair = (chip * 2 + 1 - core, me)
    right = (lax.rem(chip + 1, CHIPS) * 2 + core, me)
    left = (lax.rem(chip + CHIPS - 1, CHIPS) * 2 + core, me)

    def partner(step):
        away = jnp.where(step % 2 == 0, step // 2 + 1, PARTS - (step + 1) // 2)
        return lax.rem(me + away, PARTS)

    barrier = pltpu.get_barrier_semaphore()

    @pl.loop(0, PARTS - 1)
    def _(step):
        pl.semaphore_signal(barrier, inc=1, device_id=(me_dp, partner(PARTS - 2 - step)), device_id_type=MESH)

    for other in (pair, right, left):
        pl.semaphore_signal(barrier, inc=1, device_id=other, device_id_type=MESH)

    loads = [
        pltpu.make_async_copy(source, target, load_sem.at[n])
        for n, (source, target) in enumerate(
            [
                (h_hbm, h_in), (k_hbm, k_in), (v_hbm, v_in), (q_hbm, q_in),
                (first_hbm, first), (twist_hbm, twist), (second_hbm, second),
                (second_back_hbm, second_back), (first_back_hbm, first_back),
            ]
        )
    ]
    for load in loads:
        load.start()

    def remote(source, target, sems, n, device):
        return pltpu.make_async_remote_copy(
            src_ref=source, dst_ref=target, send_sem=sems.at[(0, *n)], recv_sem=sems.at[(1, *n)],
            device_id=device, device_id_type=MESH,
        )

    loads[0].wait()

    @pl.loop(0, CUTS)
    def _(cut):
        rows = pl.ds(pl.multiple_of(cut * SIDE, SIDE), SIDE)
        for tile in range(CHANNELS // SIDE):
            lanes = slice(tile * SIDE, (tile + 1) * SIDE)
            turned_h[cut, lanes, :] = h_in[rows, lanes].astype(F32).T

    pl.semaphore_wait(barrier, PARTS - 1 + 3)

    rims = [
        remote(hbm.at[pl.ds(ROWS - 16, 16)], rim.at[n], rim_sems, (n,), (me_dp, lax.rem(me + 1, PARTS)))
        for n, hbm in enumerate([q_hbm, k_hbm, v_hbm])
    ]
    for copy in rims:
        copy.start()

    def send_chunk(turned, send, recv, sems, chunk):
        def packed(device):
            first_row = chunk * PARTS * CHUNK + device * CHUNK
            rows = pl.ds(pl.multiple_of(first_row, CHUNK), CHUNK)
            return jnp.concatenate([turned[cut, rows, :] for cut in range(CUTS)], axis=0).astype(BF16)

        @pl.loop(0, PARTS - 1)
        def _(step):
            to = partner(step)
            send[chunk, to] = packed(to)
            remote(send.at[chunk, to], recv.at[chunk, me], sems, (chunk,), (me_dp, to)).start()

        recv[chunk, me] = packed(me)
        some = pl.ds(0, PARTS - 1)
        return remote(
            send.at[chunk, some], recv.at[chunk, some], sems, (chunk,), (me_dp, lax.rem(me + 1, PARTS))
        )

    h_all, x_all = {}, {}
    h_all[0] = send_chunk(turned_h, h_send, h_recv, h_sems, 0)

    def widen(source, target, stream):
        target[0:8, :] = jnp.where(me > 0, rim[stream].astype(F32)[8:16, :], 0.0)
        target[8 : 8 + ROWS, :] = source[...].astype(F32)

    def short(wide, stream, cut, lanes):
        window = wide[pl.ds(pl.multiple_of(cut * SIDE, SIDE), SIDE + 8), lanes]
        return (
            taps_ref[stream, 0:1, lanes] * window[8:]
            + taps_ref[stream, 1:2, lanes] * window[7:-1]
            + taps_ref[stream, 2:3, lanes] * window[6:-2]
        )

    loads[1].wait()
    loads[2].wait()
    rims[1].wait()
    rims[2].wait()
    widen(k_in, wide_k, 1)
    widen(v_in, wide_v, 2)

    @pl.loop(0, CUTS)
    def _(cut):
        rows = pl.ds(pl.multiple_of(cut * SIDE, SIDE), SIDE)
        for tile in range(CHANNELS // SIDE):
            lanes = slice(tile * SIDE, (tile + 1) * SIDE)
            value = (short(wide_k, 1, cut, lanes) * short(wide_v, 2, cut, lanes)).astype(BF16)
            mixed[rows, lanes] = value
            turned_x[cut, lanes, :] = value.astype(F32).T

    x_all[0] = send_chunk(turned_x, x_send, x_recv, x_sems, 0)

    def columns(chip_to, core_to):
        return pl.ds(pl.multiple_of((chip_to * 2 + core_to) * COLUMNS, COLUMNS), COLUMNS)

    w_loads = [
        pltpu.make_async_copy(w_hbm.at[:, columns(n, core)], w_all.at[core, n], w_load_sem.at[n])
        for n in range(CHIPS)
    ]
    w_sent = [
        remote(w_hbm.at[:, columns(n, 1 - core)], w_all.at[core, n], w_sems, (n,), pair)
        for n in range(CHIPS)
    ]
    for copy in w_loads + w_sent:
        copy.start()

    loads[3].wait()
    rims[0].wait()
    widen(q_in, wide_k, 0)

    @pl.loop(0, CUTS)
    def _(cut):
        rows = pl.ds(pl.multiple_of(cut * SIDE, SIDE), SIDE)
        for tile in range(CHANNELS // SIDE):
            lanes = slice(tile * SIDE, (tile + 1) * SIDE)
            queries[rows, lanes] = short(wide_k, 0, cut, lanes)

    def spectrum(base):
        data = jnp.concatenate(
            [flat[pl.ds(base + n, SIDE, stride=CHUNK), :] for n in range(2)], axis=1
        ).astype(BF16)
        part = jnp.dot(first[...], jnp.concatenate([data, data], axis=0), preferred_element_type=F32)
        rows = []
        for n in range(2):
            lanes = slice(n * SIDE, (n + 1) * SIDE)
            real, imag = part[:SIDE, lanes], part[SIDE:, lanes]
            rows.append(
                jnp.concatenate(
                    [real * twist[0] - imag * twist[1], real * twist[1] + imag * twist[0]], axis=1
                )
            )
        high, low = split(jnp.concatenate(rows, axis=0))
        return jnp.dot(
            jnp.concatenate([high, low, high], axis=1), second[...], preferred_element_type=F32
        )

    def unpack(arrived, chunk):
        @pl.loop(0, PARTS)
        def _(source):
            rows = pl.ds(pl.multiple_of(source * CUTS * CHUNK, CUTS * CHUNK), CUTS * CHUNK)
            flat[rows, :] = arrived[chunk, source].astype(F32)

    def filter_spectra(chunk):
        h_all[chunk].wait_recv()
        unpack(h_recv, chunk)

        @pl.loop(0, CHUNK // 2)
        def _(step):
            spectra[chunk * (CHUNK // 2) + step] = spectrum(step * 2)

    def convolve(chunk):
        x_all[chunk].wait_recv()
        unpack(x_recv, chunk)

        @pl.loop(0, CHUNK // 2)
        def _(step):
            x_spec = spectrum(step * 2)
            h_spec = spectra[chunk * (CHUNK // 2) + step]
            x_real, x_imag = x_spec[:, :SIDE], x_spec[:, SIDE:]
            h_real, h_imag = h_spec[:, :SIDE], h_spec[:, SIDE:]
            high, low = split(
                jnp.concatenate(
                    [x_real * h_real - x_imag * h_imag, x_real * h_imag + x_imag * h_real], axis=1
                )
            )
            product = jnp.dot(
                jnp.concatenate([high, low, high], axis=1),
                second_back[...],
                preferred_element_type=F32,
            )
            stacked = []
            for n in range(2):
                rows = slice(n * SIDE, (n + 1) * SIDE)
                real, imag = product[rows, :SIDE], product[rows, SIDE:]
                high, low = split(
                    jnp.concatenate(
                        [real * twist[0] + imag * twist[1], imag * twist[0] - real * twist[1]], axis=0
                    )
                )
                stacked.append(jnp.concatenate([high, low, high], axis=0))
            values = jnp.dot(
                first_back[...], jnp.concatenate(stacked, axis=1), preferred_element_type=F32
            )
            for n in range(2):
                y_flat[pl.ds(step * 2 + n, SIDE, stride=CHUNK), :] = values[:, n * SIDE : (n + 1) * SIDE]

        @pl.loop(0, PARTS)
        def _(device):
            rows = pl.ds(pl.multiple_of(device * CUTS * CHUNK, CUTS * CHUNK), CUTS * CHUNK)
            value = y_flat[rows, :].astype(BF16)
            for half in range(2):
                y_send[chunk, half, device] = value[half * 16 : (half + 1) * 16]

    def send_back(chunk, half):
        @pl.loop(0, PARTS - 1)
        def _(step):
            to = partner(step)
            remote(
                y_send.at[chunk, half, to], y_recv.at[chunk, half, me], y_sems, (chunk, half),
                (me_dp, to),
            ).start()

        y_recv[chunk, half, me] = y_send[chunk, half, me]
        some = pl.ds(0, PARTS - 1)
        return remote(
            y_send.at[chunk, half, some], y_recv.at[chunk, half, some], y_sems, (chunk, half),
            (me_dp, lax.rem(me + 1, PARTS)),
        )

    for load in loads[4:]:
        load.wait()
    y_all = {}
    h_all[0].wait_send()
    h_all[1] = send_chunk(turned_h, h_send, h_recv, h_sems, 1)
    filter_spectra(0)
    x_all[0].wait_send()
    x_all[1] = send_chunk(turned_x, x_send, x_recv, x_sems, 1)
    convolve(0)
    y_all[0, 0] = send_back(0, 0)
    filter_spectra(1)
    convolve(1)
    y_all[1, 0] = send_back(1, 0)

    def gate(chunk, half):
        y_all[chunk, half].wait_recv()

        @pl.loop(0, PARTS)
        def _(source):
            value = y_recv[chunk, half, source].astype(F32)
            rows = pl.ds(pl.multiple_of(source * CHUNK, CHUNK), CHUNK)
            for n in range(2):
                back[n, rows, :] = value[n * CHUNK : (n + 1) * CHUNK, :]

        @pl.loop(0, 2)
        def _(n):
            rows = pl.ds(pl.multiple_of(half * HALF + n * SIDE, SIDE), SIDE)
            for tile in range(PARTS * CHUNK // SIDE):
                first_lane = chunk * PARTS * CHUNK + tile * SIDE
                lanes = slice(first_lane, first_lane + SIDE)
                convolved = back[n, tile * SIDE : (tile + 1) * SIDE, :].T
                direct = skip_ref[0:1, lanes] * mixed[rows, lanes].astype(F32)
                gated[core, rows, lanes] = (queries[rows, lanes] * (convolved + direct)).astype(BF16)

        lanes = pl.ds(chunk * PARTS * CHUNK, PARTS * CHUNK)
        block = gated.at[core, pl.ds(half * HALF, HALF), lanes]
        copy = remote(block, block, gated_sems, (chunk, half), pair)
        copy.start()
        return copy

    def partial(half, to, strip):
        rows, lanes = slice(half * HALF, (half + 1) * HALF), slice(strip * STRIP, (strip + 1) * STRIP)
        return jnp.dot(
            gated[0, rows, :], w_all[0, to, :, lanes], preferred_element_type=F32
        ) + jnp.dot(gated[1, rows, :], w_all[1, to, :, lanes], preferred_element_type=F32)

    chip_right, chip_left = lax.rem(chip + 1, CHIPS), lax.rem(chip + CHIPS - 1, CHIPS)
    chip_across = lax.rem(chip + 2, CHIPS)
    far, near = {}, {}
    ways = ((0, right, chip_right), (1, left, chip_left))

    def send_far(half):
        for way, device, _ in ways:
            far_send[half, way] = partial(half, chip_across, way).astype(BF16)
            far[half, way] = remote(
                far_send.at[half, way], far_recv.at[half, way], far_sems, (half, way), device
            )
            far[half, way].start()

    def send_near(half, passed):
        for way, device, to in ways:
            strip = way if passed else 1 - way
            value = partial(half, to, strip)
            if passed:
                far[half, way].wait_recv()
                value = value + far_recv[half, way].astype(F32)
            near_send[half, way, strip] = value.astype(BF16)
            near[half, way, strip] = remote(
                near_send.at[half, way, strip], near_recv.at[half, way, strip], near_sems,
                (half, way, strip), device,
            )
            near[half, way, strip].start()

    def finish(half):
        for strip in range(2):
            value = partial(half, chip, strip)
            for way in range(2):
                near[half, way, strip].wait_recv()
                value = value + near_recv[half, way, strip].astype(F32)
            out_ref[half * HALF : (half + 1) * HALF, strip * STRIP : (strip + 1) * STRIP] = value.astype(BF16)

    exchanged = [gate(0, 0)]
    y_all[1, 0].wait_send()
    y_all[0, 1] = send_back(0, 1)
    y_all[1, 1] = send_back(1, 1)
    exchanged.append(gate(1, 0))
    for copy in w_loads + w_sent + exchanged:
        copy.wait()
    send_far(0)
    send_near(0, False)
    exchanged = [gate(0, 1)]
    send_near(0, True)
    exchanged.append(gate(1, 1))
    for copy in exchanged:
        copy.wait()
    send_far(1)
    send_near(1, False)
    finish(0)
    send_near(1, True)
    finish(1)

    y_all[0, 0].wait_send()
    for copy in [h_all[1], x_all[1], y_all[0, 1], y_all[1, 1], *far.values(), *near.values()]:
        copy.wait_send()


def body(q_proj, k_proj, v_proj, short_taps, long_filter, skip_gain, w_out):
    constants = [jnp.asarray(t) for t in tables(SIDE)]
    wide = (8 + ROWS, CHANNELS)
    stream = (ROWS, CHANNELS)
    travel = (2, PARTS, CUTS * CHUNK, SIDE)
    pieces = (2, 2, PARTS, 16, SIDE)
    dma = pltpu.SemaphoreType.DMA
    anywhere = pl.BlockSpec(memory_space=pl.ANY)
    local = pl.BlockSpec(memory_space=pltpu.VMEM)
    return pl.pallas_call(
        kernel,
        out_shape=jax.ShapeDtypeStruct((ROWS, COLUMNS), BF16),
        in_specs=[anywhere] * 5 + [local] * 2 + [anywhere] * 5,
        out_specs=local,
        scratch_shapes=[
            *[pltpu.VMEM(stream, BF16)] * 4,
            pltpu.VMEM((2, CHIPS, CHANNELS, COLUMNS), BF16),
            *[pltpu.VMEM(t.shape, t.dtype) for t in constants],
            pltpu.VMEM((3, 16, CHANNELS), BF16),
            pltpu.VMEM(wide, F32),
            pltpu.VMEM(wide, F32),
            *[pltpu.VMEM((CUTS, CHANNELS, SIDE), F32)] * 2,
            pltpu.VMEM(stream, BF16),
            pltpu.VMEM(stream, F32),
            *[pltpu.VMEM(travel, BF16)] * 4,
            pltpu.VMEM((SIDE * CHUNK, SIDE), F32),
            pltpu.VMEM((CHUNK, 2 * SIDE, 2 * SIDE), F32),
            pltpu.VMEM((SIDE * CHUNK, SIDE), F32),
            *[pltpu.VMEM(pieces, BF16)] * 2,
            pltpu.VMEM((2, PARTS * CHUNK, SIDE), F32),
            pltpu.VMEM((2, ROWS, CHANNELS), BF16),
            *[pltpu.VMEM((2, 2, HALF, STRIP), BF16)] * 2,
            *[pltpu.VMEM((2, 2, 2, HALF, STRIP), BF16)] * 2,
            dma((9,)),
            dma((2, 3)),
            dma((CHIPS,)),
            dma((2, CHIPS)),
            dma((2, 2)),
            dma((2, 2)),
            dma((2, 2, 2)),
            dma((2, 2, 2)),
            dma((2, 2, 2)),
            dma((2, 2, 2, 2)),
        ],
        compiler_params=pltpu.CompilerParams(
            collective_id=0, has_side_effects=True, vmem_limit_bytes=56 * 1024 * 1024
        ),
    )(
        q_proj, k_proj, v_proj, long_filter, w_out, short_taps, skip_gain[None, :], *constants
    )


def solution(mesh):
    placed = (
        P("ctx", "dp"),
        P("ctx", "dp"),
        P("ctx", "dp"),
        P(None, None, "dp"),
        P("ctx", "dp"),
        P("dp"),
        P("dp", None),
    )
    return jax.shard_map(
        body, mesh=mesh, in_specs=placed, out_specs=P("ctx", "dp"), check_vma=False
    )
```

```python
import functools
import math

import jax
import jax.numpy as jnp
import ml_dtypes
import numpy as np
from jax import lax
from jax.experimental import pallas as pl
from jax.experimental.pallas import tpu as pltpu
from jax.sharding import PartitionSpec as P

BF16 = jnp.bfloat16
F32 = jnp.float32
MESH = pl.DeviceIdType.MESH

ROWS = 512
CHANNELS = 512
PARTS = 32
CHIPS = 4
SIDE = 128
CUTS = ROWS // SIDE
CHUNK = 8
COLUMNS = 512
HALF = ROWS // 2
STRIP = COLUMNS // 2


def halves(table):
    high = table.astype(ml_dtypes.bfloat16)
    low = (table - high.astype(np.float64)).astype(ml_dtypes.bfloat16)
    return high, low


@functools.lru_cache(None)
def tables(side):
    total = side * side
    index = np.arange(side)
    quarter = index + 0.25
    outer = -2.0 * math.pi * quarter[:, None] * index[None, :] / side
    high, low = halves(np.concatenate([np.cos(outer), np.sin(outer)], axis=0))
    first = np.concatenate([high, low], axis=1)
    turn = -2.0 * math.pi * quarter[:, None] * index[None, :] / total
    twist = np.stack([np.cos(turn), np.sin(turn)]).astype(np.float32)
    inner = -2.0 * math.pi * index[:, None] * index[None, :] / side
    cosine, sine = np.cos(inner), np.sin(inner)
    high, low = halves(np.block([[cosine, sine], [-sine, cosine]]))
    second = np.concatenate([high, high, low], axis=0)
    high, low = halves(np.block([[cosine, -sine], [sine, cosine]]))
    second_back = np.concatenate([high, high, low], axis=0)
    high, low = halves(np.concatenate([np.cos(outer).T, np.sin(outer).T], axis=1) / total)
    first_back = np.concatenate([high, high, low], axis=1)
    return first, twist, second, second_back, first_back


def split(value):
    high = value.astype(BF16)
    low = (value - high.astype(F32)).astype(BF16)
    return high, low


def kernel(
    q_hbm, k_hbm, v_hbm, h_hbm, w_hbm, taps_ref, skip_ref,
    first_hbm, twist_hbm, second_hbm, second_back_hbm, first_back_hbm,
    out_ref,
    q_in, k_in, v_in, h_in, w_all, first, twist, second, second_back, first_back,
    rim, wide_k, wide_v, turned_h, turned_x, mixed, queries,
    h_send, h_recv, x_send, x_recv, flat, spectra, y_flat, y_send, y_recv, back,
    gated, far_send, far_recv, near_send, near_recv,
    load_sem, rim_sems, w_load_sem, w_sems, h_sems, x_sems, y_sems, gated_sems, far_sems, near_sems,
):
    me_dp, me = lax.axis_index("dp"), lax.axis_index("ctx")
    chip, core = me_dp // 2, me_dp % 2
    pair = (chip * 2 + 1 - core, me)
    right = (lax.rem(chip + 1, CHIPS) * 2 + core, me)
    left = (lax.rem(chip + CHIPS - 1, CHIPS) * 2 + core, me)

    def partner(turn):
        step = PARTS - 2 - turn
        away = jnp.where(step % 2 == 0, step // 2 + 1, PARTS - (step + 1) // 2)
        return lax.rem(me + away, PARTS)

    barrier = pltpu.get_barrier_semaphore()

    @pl.loop(0, PARTS - 1)
    def _(step):
        pl.semaphore_signal(barrier, inc=1, device_id=(me_dp, partner(step)), device_id_type=MESH)

    for other in (pair, right, left):
        pl.semaphore_signal(barrier, inc=1, device_id=other, device_id_type=MESH)

    loads = [
        pltpu.make_async_copy(source, target, load_sem.at[n])
        for n, (source, target) in enumerate(
            [
                (h_hbm, h_in), (k_hbm, k_in), (v_hbm, v_in), (q_hbm, q_in),
                (first_hbm, first), (twist_hbm, twist), (second_hbm, second),
                (second_back_hbm, second_back), (first_back_hbm, first_back),
            ]
        )
    ]
    for load in loads:
        load.start()

    def remote(source, target, sems, n, device):
        return pltpu.make_async_remote_copy(
            src_ref=source, dst_ref=target, send_sem=sems.at[(0, *n)], recv_sem=sems.at[(1, *n)],
            device_id=device, device_id_type=MESH,
        )

    loads[0].wait()

    @pl.loop(0, CUTS)
    def _(cut):
        rows = pl.ds(pl.multiple_of(cut * SIDE, SIDE), SIDE)
        for tile in range(CHANNELS // SIDE):
            lanes = slice(tile * SIDE, (tile + 1) * SIDE)
            turned_h[cut, lanes, :] = h_in[rows, lanes].astype(F32).T

    pl.semaphore_wait(barrier, PARTS - 1 + 3)

    rims = [
        remote(hbm.at[pl.ds(ROWS - 16, 16)], rim.at[n], rim_sems, (n,), (me_dp, lax.rem(me + 1, PARTS)))
        for n, hbm in enumerate([q_hbm, k_hbm, v_hbm])
    ]
    for copy in rims:
        copy.start()

    def send_chunk(turned, send, recv, sems, chunk):
        def packed(device):
            first_row = chunk * PARTS * CHUNK + device * CHUNK
            rows = pl.ds(pl.multiple_of(first_row, CHUNK), CHUNK)
            return jnp.concatenate([turned[cut, rows, :] for cut in range(CUTS)], axis=0).astype(BF16)

        @pl.loop(0, PARTS - 1)
        def _(step):
            to = partner(step)
            send[chunk, to] = packed(to)
            remote(send.at[chunk, to], recv.at[chunk, me], sems, (chunk,), (me_dp, to)).start()

        recv[chunk, me] = packed(me)
        some = pl.ds(0, PARTS - 1)
        return remote(
            send.at[chunk, some], recv.at[chunk, some], sems, (chunk,), (me_dp, lax.rem(me + 1, PARTS))
        )

    h_all, x_all = {}, {}
    h_all[0] = send_chunk(turned_h, h_send, h_recv, h_sems, 0)

    def widen(source, target, stream):
        target[0:8, :] = jnp.where(me > 0, rim[stream].astype(F32)[8:16, :], 0.0)
        target[8 : 8 + ROWS, :] = source[...].astype(F32)

    def short(wide, stream, cut, lanes):
        window = wide[pl.ds(pl.multiple_of(cut * SIDE, SIDE), SIDE + 8), lanes]
        return (
            taps_ref[stream, 0:1, lanes] * window[8:]
            + taps_ref[stream, 1:2, lanes] * window[7:-1]
            + taps_ref[stream, 2:3, lanes] * window[6:-2]
        )

    loads[1].wait()
    loads[2].wait()
    rims[1].wait()
    rims[2].wait()
    widen(k_in, wide_k, 1)
    widen(v_in, wide_v, 2)

    @pl.loop(0, CUTS)
    def _(cut):
        rows = pl.ds(pl.multiple_of(cut * SIDE, SIDE), SIDE)
        for tile in range(CHANNELS // SIDE):
            lanes = slice(tile * SIDE, (tile + 1) * SIDE)
            value = (short(wide_k, 1, cut, lanes) * short(wide_v, 2, cut, lanes)).astype(BF16)
            mixed[rows, lanes] = value
            turned_x[cut, lanes, :] = value.astype(F32).T

    x_all[0] = send_chunk(turned_x, x_send, x_recv, x_sems, 0)

    def columns(chip_to, core_to):
        return pl.ds(pl.multiple_of((chip_to * 2 + core_to) * COLUMNS, COLUMNS), COLUMNS)

    w_loads = [
        pltpu.make_async_copy(w_hbm.at[:, columns(n, core)], w_all.at[core, n], w_load_sem.at[n])
        for n in range(CHIPS)
    ]
    w_sent = [
        remote(w_hbm.at[:, columns(n, 1 - core)], w_all.at[core, n], w_sems, (n,), pair)
        for n in range(CHIPS)
    ]
    for copy in w_loads + w_sent:
        copy.start()

    loads[3].wait()
    rims[0].wait()
    widen(q_in, wide_k, 0)

    @pl.loop(0, CUTS)
    def _(cut):
        rows = pl.ds(pl.multiple_of(cut * SIDE, SIDE), SIDE)
        for tile in range(CHANNELS // SIDE):
            lanes = slice(tile * SIDE, (tile + 1) * SIDE)
            queries[rows, lanes] = short(wide_k, 0, cut, lanes)

    def spectrum(base):
        data = jnp.concatenate(
            [flat[pl.ds(base + n, SIDE, stride=CHUNK), :] for n in range(2)], axis=1
        ).astype(BF16)
        part = jnp.dot(first[...], jnp.concatenate([data, data], axis=0), preferred_element_type=F32)
        rows = []
        for n in range(2):
            lanes = slice(n * SIDE, (n + 1) * SIDE)
            real, imag = part[:SIDE, lanes], part[SIDE:, lanes]
            rows.append(
                jnp.concatenate(
                    [real * twist[0] - imag * twist[1], real * twist[1] + imag * twist[0]], axis=1
                )
            )
        high, low = split(jnp.concatenate(rows, axis=0))
        return jnp.dot(
            jnp.concatenate([high, low, high], axis=1), second[...], preferred_element_type=F32
        )

    def unpack(arrived, chunk):
        @pl.loop(0, PARTS)
        def _(source):
            rows = pl.ds(pl.multiple_of(source * CUTS * CHUNK, CUTS * CHUNK), CUTS * CHUNK)
            flat[rows, :] = arrived[chunk, source].astype(F32)

    def filter_spectra(chunk):
        h_all[chunk].wait_recv()
        unpack(h_recv, chunk)

        for step in range(CHUNK // 2):
            spectra[chunk * (CHUNK // 2) + step] = spectrum(step * 2)

    def convolve(chunk):
        x_all[chunk].wait_recv()
        unpack(x_recv, chunk)

        def invert(x_spec, step):
            h_spec = spectra[chunk * (CHUNK // 2) + step]
            x_real, x_imag = x_spec[:, :SIDE], x_spec[:, SIDE:]
            h_real, h_imag = h_spec[:, :SIDE], h_spec[:, SIDE:]
            high, low = split(
                jnp.concatenate(
                    [x_real * h_real - x_imag * h_imag, x_real * h_imag + x_imag * h_real], axis=1
                )
            )
            product = jnp.dot(
                jnp.concatenate([high, low, high], axis=1),
                second_back[...],
                preferred_element_type=F32,
            )
            stacked = []
            for n in range(2):
                rows = slice(n * SIDE, (n + 1) * SIDE)
                real, imag = product[rows, :SIDE], product[rows, SIDE:]
                high, low = split(
                    jnp.concatenate(
                        [real * twist[0] + imag * twist[1], imag * twist[0] - real * twist[1]], axis=0
                    )
                )
                stacked.append(jnp.concatenate([high, low, high], axis=0))
            values = jnp.dot(
                first_back[...], jnp.concatenate(stacked, axis=1), preferred_element_type=F32
            )
            for n in range(2):
                y_flat[pl.ds(step * 2 + n, SIDE, stride=CHUNK), :] = values[:, n * SIDE : (n + 1) * SIDE]

        x_spec = spectrum(0)
        for step in range(CHUNK // 2):
            later = spectrum(step * 2 + 2) if step + 1 < CHUNK // 2 else None
            invert(x_spec, step)
            x_spec = later

        @pl.loop(0, PARTS)
        def _(device):
            rows = pl.ds(pl.multiple_of(device * CUTS * CHUNK, CUTS * CHUNK), CUTS * CHUNK)
            value = y_flat[rows, :].astype(BF16)
            for half in range(2):
                y_send[chunk, half, device] = value[half * 16 : (half + 1) * 16]

    def send_back(chunk, half):
        @pl.loop(0, PARTS - 1)
        def _(step):
            to = partner(step)
            remote(
                y_send.at[chunk, half, to], y_recv.at[chunk, half, me], y_sems, (chunk, half),
                (me_dp, to),
            ).start()

        y_recv[chunk, half, me] = y_send[chunk, half, me]
        some = pl.ds(0, PARTS - 1)
        return remote(
            y_send.at[chunk, half, some], y_recv.at[chunk, half, some], y_sems, (chunk, half),
            (me_dp, lax.rem(me + 1, PARTS)),
        )

    for load in loads[4:]:
        load.wait()
    y_all = {}
    h_all[0].wait_send()
    h_all[1] = send_chunk(turned_h, h_send, h_recv, h_sems, 1)
    filter_spectra(0)
    x_all[0].wait_send()
    x_all[1] = send_chunk(turned_x, x_send, x_recv, x_sems, 1)
    convolve(0)
    y_all[0, 0] = send_back(0, 0)
    filter_spectra(1)
    convolve(1)
    y_all[1, 0] = send_back(1, 0)

    def gate(chunk, half):
        y_all[chunk, half].wait_recv()

        @pl.loop(0, PARTS)
        def _(source):
            value = y_recv[chunk, half, source].astype(F32)
            rows = pl.ds(pl.multiple_of(source * CHUNK, CHUNK), CHUNK)
            for n in range(2):
                back[n, rows, :] = value[n * CHUNK : (n + 1) * CHUNK, :]

        @pl.loop(0, 2)
        def _(n):
            rows = pl.ds(pl.multiple_of(half * HALF + n * SIDE, SIDE), SIDE)
            for tile in range(PARTS * CHUNK // SIDE):
                first_lane = chunk * PARTS * CHUNK + tile * SIDE
                lanes = slice(first_lane, first_lane + SIDE)
                convolved = back[n, tile * SIDE : (tile + 1) * SIDE, :].T
                direct = skip_ref[0:1, lanes] * mixed[rows, lanes].astype(F32)
                gated[core, rows, lanes] = (queries[rows, lanes] * (convolved + direct)).astype(BF16)

        lanes = pl.ds(chunk * PARTS * CHUNK, PARTS * CHUNK)
        block = gated.at[core, pl.ds(half * HALF, HALF), lanes]
        copy = remote(block, block, gated_sems, (chunk, half), pair)
        copy.start()
        return copy

    def partial(half, to, strip):
        rows, lanes = slice(half * HALF, (half + 1) * HALF), slice(strip * STRIP, (strip + 1) * STRIP)
        return jnp.dot(
            gated[0, rows, :], w_all[0, to, :, lanes], preferred_element_type=F32
        ) + jnp.dot(gated[1, rows, :], w_all[1, to, :, lanes], preferred_element_type=F32)

    chip_right, chip_left = lax.rem(chip + 1, CHIPS), lax.rem(chip + CHIPS - 1, CHIPS)
    chip_across = lax.rem(chip + 2, CHIPS)
    far, near = {}, {}
    ways = ((0, right, chip_right), (1, left, chip_left))

    def send_far(half):
        for way, device, _ in ways:
            far_send[half, way] = partial(half, chip_across, way).astype(BF16)
            far[half, way] = remote(
                far_send.at[half, way], far_recv.at[half, way], far_sems, (half, way), device
            )
            far[half, way].start()

    def send_near(half, passed):
        for way, device, to in ways:
            strip = way if passed else 1 - way
            value = partial(half, to, strip)
            if passed:
                far[half, way].wait_recv()
                value = value + far_recv[half, way].astype(F32)
            near_send[half, way, strip] = value.astype(BF16)
            near[half, way, strip] = remote(
                near_send.at[half, way, strip], near_recv.at[half, way, strip], near_sems,
                (half, way, strip), device,
            )
            near[half, way, strip].start()

    def finish(half):
        for strip in range(2):
            value = partial(half, chip, strip)
            for way in range(2):
                near[half, way, strip].wait_recv()
                value = value + near_recv[half, way, strip].astype(F32)
            out_ref[half * HALF : (half + 1) * HALF, strip * STRIP : (strip + 1) * STRIP] = value.astype(BF16)

    exchanged = [gate(0, 0)]
    y_all[1, 0].wait_send()
    y_all[0, 1] = send_back(0, 1)
    y_all[1, 1] = send_back(1, 1)
    exchanged.append(gate(1, 0))
    for copy in w_loads + w_sent + exchanged:
        copy.wait()
    send_far(0)
    send_near(0, False)
    exchanged = [gate(0, 1)]
    send_near(0, True)
    exchanged.append(gate(1, 1))
    for copy in exchanged:
        copy.wait()
    send_far(1)
    send_near(1, False)
    finish(0)
    send_near(1, True)
    finish(1)

    y_all[0, 0].wait_send()
    for copy in [h_all[1], x_all[1], y_all[0, 1], y_all[1, 1], *far.values(), *near.values()]:
        copy.wait_send()


def body(q_proj, k_proj, v_proj, short_taps, long_filter, skip_gain, w_out):
    constants = [jnp.asarray(t) for t in tables(SIDE)]
    wide = (8 + ROWS, CHANNELS)
    stream = (ROWS, CHANNELS)
    travel = (2, PARTS, CUTS * CHUNK, SIDE)
    pieces = (2, 2, PARTS, 16, SIDE)
    dma = pltpu.SemaphoreType.DMA
    anywhere = pl.BlockSpec(memory_space=pl.ANY)
    local = pl.BlockSpec(memory_space=pltpu.VMEM)
    return pl.pallas_call(
        kernel,
        out_shape=jax.ShapeDtypeStruct((ROWS, COLUMNS), BF16),
        in_specs=[anywhere] * 5 + [local] * 2 + [anywhere] * 5,
        out_specs=local,
        scratch_shapes=[
            *[pltpu.VMEM(stream, BF16)] * 4,
            pltpu.VMEM((2, CHIPS, CHANNELS, COLUMNS), BF16),
            *[pltpu.VMEM(t.shape, t.dtype) for t in constants],
            pltpu.VMEM((3, 16, CHANNELS), BF16),
            pltpu.VMEM(wide, F32),
            pltpu.VMEM(wide, F32),
            *[pltpu.VMEM((CUTS, CHANNELS, SIDE), F32)] * 2,
            pltpu.VMEM(stream, BF16),
            pltpu.VMEM(stream, F32),
            *[pltpu.VMEM(travel, BF16)] * 4,
            pltpu.VMEM((SIDE * CHUNK, SIDE), F32),
            pltpu.VMEM((CHUNK, 2 * SIDE, 2 * SIDE), F32),
            pltpu.VMEM((SIDE * CHUNK, SIDE), F32),
            *[pltpu.VMEM(pieces, BF16)] * 2,
            pltpu.VMEM((2, PARTS * CHUNK, SIDE), F32),
            pltpu.VMEM((2, ROWS, CHANNELS), BF16),
            *[pltpu.VMEM((2, 2, HALF, STRIP), BF16)] * 2,
            *[pltpu.VMEM((2, 2, 2, HALF, STRIP), BF16)] * 2,
            dma((9,)),
            dma((2, 3)),
            dma((CHIPS,)),
            dma((2, CHIPS)),
            dma((2, 2)),
            dma((2, 2)),
            dma((2, 2, 2)),
            dma((2, 2, 2)),
            dma((2, 2, 2)),
            dma((2, 2, 2, 2)),
        ],
        compiler_params=pltpu.CompilerParams(
            collective_id=0, has_side_effects=True, vmem_limit_bytes=56 * 1024 * 1024
        ),
    )(
        q_proj, k_proj, v_proj, long_filter, w_out, short_taps, skip_gain[None, :], *constants
    )


def solution(mesh):
    placed = (
        P("ctx", "dp"),
        P("ctx", "dp"),
        P("ctx", "dp"),
        P(None, None, "dp"),
        P("ctx", "dp"),
        P("dp"),
        P("dp", None),
    )
    return jax.shard_map(
        body, mesh=mesh, in_specs=placed, out_specs=P("ctx", "dp"), check_vma=False
    )
```

```python
import functools
import math

import jax
import jax.numpy as jnp
import ml_dtypes
import numpy as np
from jax import lax
from jax.experimental import pallas as pl
from jax.experimental.pallas import tpu as pltpu
from jax.sharding import PartitionSpec as P

BF16 = jnp.bfloat16
F32 = jnp.float32
MESH = pl.DeviceIdType.MESH

ROWS = 512
CHANNELS = 512
PARTS = 32
CHIPS = 4
SIDE = 128
CUTS = ROWS // SIDE
CHUNK = 8
COLUMNS = 512
HALF = ROWS // 2
STRIP = COLUMNS // 2


def halves(table):
    high = table.astype(ml_dtypes.bfloat16)
    low = (table - high.astype(np.float64)).astype(ml_dtypes.bfloat16)
    return high, low


@functools.lru_cache(None)
def tables(side):
    total = side * side
    index = np.arange(side)
    quarter = index + 0.25
    outer = -2.0 * math.pi * quarter[:, None] * index[None, :] / side
    high, low = halves(np.concatenate([np.cos(outer), np.sin(outer)], axis=0))
    first = np.concatenate([high, low], axis=1)
    turn = -2.0 * math.pi * quarter[:, None] * index[None, :] / total
    twist = np.stack([np.cos(turn), np.sin(turn)]).astype(np.float32)
    inner = -2.0 * math.pi * index[:, None] * index[None, :] / side
    cosine, sine = np.cos(inner), np.sin(inner)
    high, low = halves(np.block([[cosine, sine], [-sine, cosine]]))
    second = np.concatenate([high, high, low], axis=0)
    high, low = halves(np.block([[cosine, -sine], [sine, cosine]]))
    second_back = np.concatenate([high, high, low], axis=0)
    high, low = halves(np.concatenate([np.cos(outer).T, np.sin(outer).T], axis=1) / total)
    first_back = np.concatenate([high, high, low], axis=1)
    return first, twist, second, second_back, first_back


def split(value):
    high = value.astype(BF16)
    low = (value - high.astype(F32)).astype(BF16)
    return high, low


def kernel(
    q_hbm, k_hbm, v_hbm, h_hbm, w_hbm, taps_ref, skip_ref,
    first_hbm, twist_hbm, second_hbm, second_back_hbm, first_back_hbm,
    out_ref,
    q_in, k_in, v_in, h_in, w_all, first, twist, second, second_back, first_back,
    rim, wide_k, wide_v, turned_h, turned_x, mixed, queries,
    h_send, h_recv, x_send, x_recv, flat, spectra, y_flat, y_send, y_recv, back,
    gated, far_send, far_recv, near_send, near_recv,
    load_sem, rim_sems, w_load_sem, w_sems, h_sems, x_sems, y_sems, gated_sems, far_sems, near_sems,
):
    me_dp, me = lax.axis_index("dp"), lax.axis_index("ctx")
    chip, core = me_dp // 2, me_dp % 2
    pair = (chip * 2 + 1 - core, me)
    right = (lax.rem(chip + 1, CHIPS) * 2 + core, me)
    left = (lax.rem(chip + CHIPS - 1, CHIPS) * 2 + core, me)

    def partner(turn):
        step = PARTS - 2 - turn
        away = jnp.where(step % 2 == 0, step // 2 + 1, PARTS - (step + 1) // 2)
        return lax.rem(me + away, PARTS)

    barrier = pltpu.get_barrier_semaphore()

    @pl.loop(0, PARTS - 1)
    def _(step):
        pl.semaphore_signal(barrier, inc=1, device_id=(me_dp, partner(step)), device_id_type=MESH)

    for other in (pair, right, left):
        pl.semaphore_signal(barrier, inc=1, device_id=other, device_id_type=MESH)

    loads = [
        pltpu.make_async_copy(source, target, load_sem.at[n])
        for n, (source, target) in enumerate(
            [
                (h_hbm, h_in), (k_hbm, k_in), (v_hbm, v_in), (q_hbm, q_in),
                (first_hbm, first), (twist_hbm, twist), (second_hbm, second),
                (second_back_hbm, second_back), (first_back_hbm, first_back),
            ]
        )
    ]
    for load in loads:
        load.start()

    def remote(source, target, sems, n, device):
        return pltpu.make_async_remote_copy(
            src_ref=source, dst_ref=target, send_sem=sems.at[(0, *n)], recv_sem=sems.at[(1, *n)],
            device_id=device, device_id_type=MESH,
        )

    loads[0].wait()

    @pl.loop(0, CUTS)
    def _(cut):
        rows = pl.ds(pl.multiple_of(cut * SIDE, SIDE), SIDE)
        for tile in range(CHANNELS // SIDE):
            lanes = slice(tile * SIDE, (tile + 1) * SIDE)
            turned_h[cut, lanes, :] = h_in[rows, lanes].astype(F32).T

    pl.semaphore_wait(barrier, PARTS - 1 + 3)

    rims = [
        remote(hbm.at[pl.ds(ROWS - 16, 16)], rim.at[n], rim_sems, (n,), (me_dp, lax.rem(me + 1, PARTS)))
        for n, hbm in enumerate([q_hbm, k_hbm, v_hbm])
    ]
    for copy in rims:
        copy.start()

    def send_chunk(turned, send, recv, sems, chunk):
        def packed(device):
            first_row = chunk * PARTS * CHUNK + device * CHUNK
            rows = pl.ds(pl.multiple_of(first_row, CHUNK), CHUNK)
            return jnp.concatenate([turned[cut, rows, :] for cut in range(CUTS)], axis=0).astype(BF16)

        @pl.loop(0, PARTS - 1)
        def _(step):
            to = partner(step)
            send[chunk, to] = packed(to)
            remote(send.at[chunk, to], recv.at[chunk, me], sems, (chunk,), (me_dp, to)).start()

        recv[chunk, me] = packed(me)
        some = pl.ds(0, PARTS - 1)
        return remote(
            send.at[chunk, some], recv.at[chunk, some], sems, (chunk,), (me_dp, lax.rem(me + 1, PARTS))
        )

    h_all, x_all = {}, {}
    h_all[0] = send_chunk(turned_h, h_send, h_recv, h_sems, 0)

    def widen(source, target, stream):
        target[0:8, :] = jnp.where(me > 0, rim[stream].astype(F32)[8:16, :], 0.0)
        target[8 : 8 + ROWS, :] = source[...].astype(F32)

    def short(wide, stream, cut, lanes):
        window = wide[pl.ds(pl.multiple_of(cut * SIDE, SIDE), SIDE + 8), lanes]
        return (
            taps_ref[stream, 0:1, lanes] * window[8:]
            + taps_ref[stream, 1:2, lanes] * window[7:-1]
            + taps_ref[stream, 2:3, lanes] * window[6:-2]
        )

    loads[1].wait()
    loads[2].wait()
    rims[1].wait()
    rims[2].wait()
    widen(k_in, wide_k, 1)
    widen(v_in, wide_v, 2)

    @pl.loop(0, CUTS)
    def _(cut):
        rows = pl.ds(pl.multiple_of(cut * SIDE, SIDE), SIDE)
        for tile in range(CHANNELS // SIDE):
            lanes = slice(tile * SIDE, (tile + 1) * SIDE)
            value = (short(wide_k, 1, cut, lanes) * short(wide_v, 2, cut, lanes)).astype(BF16)
            mixed[rows, lanes] = value
            turned_x[cut, lanes, :] = value.astype(F32).T

    x_all[0] = send_chunk(turned_x, x_send, x_recv, x_sems, 0)

    def columns(chip_to, core_to):
        return pl.ds(pl.multiple_of((chip_to * 2 + core_to) * COLUMNS, COLUMNS), COLUMNS)

    w_loads = [
        pltpu.make_async_copy(w_hbm.at[:, columns(n, core)], w_all.at[core, n], w_load_sem.at[n])
        for n in range(CHIPS)
    ]
    w_sent = [
        remote(w_hbm.at[:, columns(n, 1 - core)], w_all.at[core, n], w_sems, (n,), pair)
        for n in range(CHIPS)
    ]
    for copy in w_loads + w_sent:
        copy.start()

    loads[3].wait()
    rims[0].wait()
    widen(q_in, wide_k, 0)

    @pl.loop(0, CUTS)
    def _(cut):
        rows = pl.ds(pl.multiple_of(cut * SIDE, SIDE), SIDE)
        for tile in range(CHANNELS // SIDE):
            lanes = slice(tile * SIDE, (tile + 1) * SIDE)
            queries[rows, lanes] = short(wide_k, 0, cut, lanes)

    def spectrum(base):
        data = jnp.concatenate(
            [flat[pl.ds(base + n, SIDE, stride=CHUNK), :] for n in range(2)], axis=1
        ).astype(BF16)
        part = jnp.dot(first[...], jnp.concatenate([data, data], axis=0), preferred_element_type=F32)
        rows = []
        for n in range(2):
            lanes = slice(n * SIDE, (n + 1) * SIDE)
            real, imag = part[:SIDE, lanes], part[SIDE:, lanes]
            rows.append(
                jnp.concatenate(
                    [real * twist[0] - imag * twist[1], real * twist[1] + imag * twist[0]], axis=1
                )
            )
        high, low = split(jnp.concatenate(rows, axis=0))
        return jnp.dot(
            jnp.concatenate([high, low, high], axis=1), second[...], preferred_element_type=F32
        )

    def unpack(arrived, chunk):
        @pl.loop(0, PARTS)
        def _(source):
            rows = pl.ds(pl.multiple_of(source * CUTS * CHUNK, CUTS * CHUNK), CUTS * CHUNK)
            flat[rows, :] = arrived[chunk, source].astype(F32)

    def filter_spectra(chunk):
        h_all[chunk].wait_recv()
        unpack(h_recv, chunk)

        for step in range(CHUNK // 2):
            spectra[chunk * (CHUNK // 2) + step] = spectrum(step * 2)

    def convolve(chunk):
        x_all[chunk].wait_recv()
        unpack(x_recv, chunk)

        def invert(x_spec, step):
            h_spec = spectra[chunk * (CHUNK // 2) + step]
            x_real, x_imag = x_spec[:, :SIDE], x_spec[:, SIDE:]
            h_real, h_imag = h_spec[:, :SIDE], h_spec[:, SIDE:]
            high, low = split(
                jnp.concatenate(
                    [x_real * h_real - x_imag * h_imag, x_real * h_imag + x_imag * h_real], axis=1
                )
            )
            product = jnp.dot(
                jnp.concatenate([high, low, high], axis=1),
                second_back[...],
                preferred_element_type=F32,
            )
            stacked = []
            for n in range(2):
                rows = slice(n * SIDE, (n + 1) * SIDE)
                real, imag = product[rows, :SIDE], product[rows, SIDE:]
                high, low = split(
                    jnp.concatenate(
                        [real * twist[0] + imag * twist[1], imag * twist[0] - real * twist[1]], axis=0
                    )
                )
                stacked.append(jnp.concatenate([high, low, high], axis=0))
            values = jnp.dot(
                first_back[...], jnp.concatenate(stacked, axis=1), preferred_element_type=F32
            )
            for n in range(2):
                y_flat[pl.ds(step * 2 + n, SIDE, stride=CHUNK), :] = values[:, n * SIDE : (n + 1) * SIDE]

        x_spec = spectrum(0)
        for step in range(CHUNK // 2):
            later = spectrum(step * 2 + 2) if step + 1 < CHUNK // 2 else None
            invert(x_spec, step)
            x_spec = later

        @pl.loop(0, PARTS)
        def _(device):
            rows = pl.ds(pl.multiple_of(device * CUTS * CHUNK, CUTS * CHUNK), CUTS * CHUNK)
            value = y_flat[rows, :].astype(BF16)
            for half in range(2):
                y_send[chunk, half, device] = value[half * 16 : (half + 1) * 16]

    def send_back(chunk, half):
        @pl.loop(0, PARTS - 1)
        def _(step):
            to = partner(step)
            remote(
                y_send.at[chunk, half, to], y_recv.at[chunk, half, me], y_sems, (chunk, half),
                (me_dp, to),
            ).start()

        y_recv[chunk, half, me] = y_send[chunk, half, me]
        some = pl.ds(0, PARTS - 1)
        return remote(
            y_send.at[chunk, half, some], y_recv.at[chunk, half, some], y_sems, (chunk, half),
            (me_dp, lax.rem(me + 1, PARTS)),
        )

    for load in loads[4:]:
        load.wait()
    y_all = {}
    h_all[0].wait_send()
    h_all[1] = send_chunk(turned_h, h_send, h_recv, h_sems, 1)
    filter_spectra(0)
    x_all[0].wait_send()
    x_all[1] = send_chunk(turned_x, x_send, x_recv, x_sems, 1)
    convolve(0)
    y_all[0, 0] = send_back(0, 0)
    filter_spectra(1)
    convolve(1)
    y_all[1, 0] = send_back(1, 0)

    def gate(chunk, half):
        y_all[chunk, half].wait_recv()

        @pl.loop(0, PARTS)
        def _(source):
            value = y_recv[chunk, half, source].astype(F32)
            rows = pl.ds(pl.multiple_of(source * CHUNK, CHUNK), CHUNK)
            for n in range(2):
                back[n, rows, :] = value[n * CHUNK : (n + 1) * CHUNK, :]

        @pl.loop(0, 2)
        def _(n):
            rows = pl.ds(pl.multiple_of(half * HALF + n * SIDE, SIDE), SIDE)
            for tile in range(PARTS * CHUNK // SIDE):
                first_lane = chunk * PARTS * CHUNK + tile * SIDE
                lanes = slice(first_lane, first_lane + SIDE)
                convolved = back[n, tile * SIDE : (tile + 1) * SIDE, :].T
                direct = skip_ref[0:1, lanes] * mixed[rows, lanes].astype(F32)
                gated[core, rows, lanes] = (queries[rows, lanes] * (convolved + direct)).astype(BF16)

        lanes = pl.ds(chunk * PARTS * CHUNK, PARTS * CHUNK)
        block = gated.at[core, pl.ds(half * HALF, HALF), lanes]
        copy = remote(block, block, gated_sems, (chunk, half), pair)
        copy.start()
        return copy

    def partial(half, to, strip):
        rows, lanes = slice(half * HALF, (half + 1) * HALF), slice(strip * STRIP, (strip + 1) * STRIP)
        return jnp.dot(
            gated[0, rows, :], w_all[0, to, :, lanes], preferred_element_type=F32
        ) + jnp.dot(gated[1, rows, :], w_all[1, to, :, lanes], preferred_element_type=F32)

    chip_right, chip_left = lax.rem(chip + 1, CHIPS), lax.rem(chip + CHIPS - 1, CHIPS)
    chip_across = lax.rem(chip + 2, CHIPS)
    far, near = {}, {}
    ways = ((0, right, chip_right), (1, left, chip_left))

    def send_far(half):
        for way, device, _ in ways:
            far_send[half, way] = partial(half, chip_across, way).astype(BF16)
            far[half, way] = remote(
                far_send.at[half, way], far_recv.at[half, way], far_sems, (half, way), device
            )
            far[half, way].start()

    def send_near(half, passed):
        for way, device, to in ways:
            strip = way if passed else 1 - way
            value = partial(half, to, strip)
            if passed:
                far[half, way].wait_recv()
                value = value + far_recv[half, way].astype(F32)
            near_send[half, way, strip] = value.astype(BF16)
            near[half, way, strip] = remote(
                near_send.at[half, way, strip], near_recv.at[half, way, strip], near_sems,
                (half, way, strip), device,
            )
            near[half, way, strip].start()

    def finish(half):
        for strip in range(2):
            value = partial(half, chip, strip)
            for way in range(2):
                near[half, way, strip].wait_recv()
                value = value + near_recv[half, way, strip].astype(F32)
            out_ref[half * HALF : (half + 1) * HALF, strip * STRIP : (strip + 1) * STRIP] = value.astype(BF16)

    exchanged = [gate(0, 0)]
    y_all[1, 0].wait_send()
    y_all[0, 1] = send_back(0, 1)
    y_all[1, 1] = send_back(1, 1)
    exchanged.append(gate(1, 0))
    for copy in w_loads + w_sent + exchanged:
        copy.wait()
    send_far(0)
    send_near(0, False)
    exchanged = [gate(0, 1), gate(1, 1)]
    for copy in exchanged:
        copy.wait()
    send_far(1)
    send_near(0, True)
    send_near(1, False)
    send_near(1, True)
    finish(0)
    finish(1)

    y_all[0, 0].wait_send()
    for copy in [h_all[1], x_all[1], y_all[0, 1], y_all[1, 1], *far.values(), *near.values()]:
        copy.wait_send()


def body(q_proj, k_proj, v_proj, short_taps, long_filter, skip_gain, w_out):
    constants = [jnp.asarray(t) for t in tables(SIDE)]
    wide = (8 + ROWS, CHANNELS)
    stream = (ROWS, CHANNELS)
    travel = (2, PARTS, CUTS * CHUNK, SIDE)
    pieces = (2, 2, PARTS, 16, SIDE)
    dma = pltpu.SemaphoreType.DMA
    anywhere = pl.BlockSpec(memory_space=pl.ANY)
    local = pl.BlockSpec(memory_space=pltpu.VMEM)
    return pl.pallas_call(
        kernel,
        out_shape=jax.ShapeDtypeStruct((ROWS, COLUMNS), BF16),
        in_specs=[anywhere] * 5 + [local] * 2 + [anywhere] * 5,
        out_specs=local,
        scratch_shapes=[
            *[pltpu.VMEM(stream, BF16)] * 4,
            pltpu.VMEM((2, CHIPS, CHANNELS, COLUMNS), BF16),
            *[pltpu.VMEM(t.shape, t.dtype) for t in constants],
            pltpu.VMEM((3, 16, CHANNELS), BF16),
            pltpu.VMEM(wide, F32),
            pltpu.VMEM(wide, F32),
            *[pltpu.VMEM((CUTS, CHANNELS, SIDE), F32)] * 2,
            pltpu.VMEM(stream, BF16),
            pltpu.VMEM(stream, F32),
            *[pltpu.VMEM(travel, BF16)] * 4,
            pltpu.VMEM((SIDE * CHUNK, SIDE), F32),
            pltpu.VMEM((CHUNK, 2 * SIDE, 2 * SIDE), F32),
            pltpu.VMEM((SIDE * CHUNK, SIDE), F32),
            *[pltpu.VMEM(pieces, BF16)] * 2,
            pltpu.VMEM((2, PARTS * CHUNK, SIDE), F32),
            pltpu.VMEM((2, ROWS, CHANNELS), BF16),
            *[pltpu.VMEM((2, 2, HALF, STRIP), BF16)] * 2,
            *[pltpu.VMEM((2, 2, 2, HALF, STRIP), BF16)] * 2,
            dma((9,)),
            dma((2, 3)),
            dma((CHIPS,)),
            dma((2, CHIPS)),
            dma((2, 2)),
            dma((2, 2)),
            dma((2, 2, 2)),
            dma((2, 2, 2)),
            dma((2, 2, 2)),
            dma((2, 2, 2, 2)),
        ],
        compiler_params=pltpu.CompilerParams(
            collective_id=0, has_side_effects=True, vmem_limit_bytes=56 * 1024 * 1024
        ),
    )(
        q_proj, k_proj, v_proj, long_filter, w_out, short_taps, skip_gain[None, :], *constants
    )


def solution(mesh):
    placed = (
        P("ctx", "dp"),
        P("ctx", "dp"),
        P("ctx", "dp"),
        P(None, None, "dp"),
        P("ctx", "dp"),
        P("dp"),
        P("dp", None),
    )
    return jax.shard_map(
        body, mesh=mesh, in_specs=placed, out_specs=P("ctx", "dp"), check_vma=False
    )
```

```python
import functools
import math

import jax
import jax.numpy as jnp
import ml_dtypes
import numpy as np
from jax import lax
from jax.experimental import pallas as pl
from jax.experimental.pallas import tpu as pltpu
from jax.sharding import PartitionSpec as P

BF16 = jnp.bfloat16
F32 = jnp.float32
MESH = pl.DeviceIdType.MESH

ROWS = 512
CHANNELS = 512
PARTS = 32
CHIPS = 4
SIDE = 128
CUTS = ROWS // SIDE
CHUNK = 8
COLUMNS = 512
HALF = ROWS // 2
STRIP = COLUMNS // 2


def halves(table):
    high = table.astype(ml_dtypes.bfloat16)
    low = (table - high.astype(np.float64)).astype(ml_dtypes.bfloat16)
    return high, low


@functools.lru_cache(None)
def tables(side):
    total = side * side
    index = np.arange(side)
    quarter = index + 0.25
    outer = -2.0 * math.pi * quarter[:, None] * index[None, :] / side
    high, low = halves(np.concatenate([np.cos(outer), np.sin(outer)], axis=0))
    first = np.concatenate([high, low], axis=1)
    turn = -2.0 * math.pi * quarter[:, None] * index[None, :] / total
    twist = np.stack([np.cos(turn), np.sin(turn)]).astype(np.float32)
    inner = -2.0 * math.pi * index[:, None] * index[None, :] / side
    cosine, sine = np.cos(inner), np.sin(inner)
    high, low = halves(np.block([[cosine, sine], [-sine, cosine]]))
    second = np.concatenate([high, high, low], axis=0)
    high, low = halves(np.block([[cosine, -sine], [sine, cosine]]))
    second_back = np.concatenate([high, high, low], axis=0)
    high, low = halves(np.concatenate([np.cos(outer).T, np.sin(outer).T], axis=1) / total)
    first_back = np.concatenate([high, high, low], axis=1)
    return first, twist, second, second_back, first_back


def split(value):
    high = value.astype(BF16)
    low = (value - high.astype(F32)).astype(BF16)
    return high, low


def kernel(
    q_hbm, k_hbm, v_hbm, h_hbm, w_hbm, taps_ref, skip_ref,
    first_hbm, twist_hbm, second_hbm, second_back_hbm, first_back_hbm,
    out_ref,
    q_in, k_in, v_in, h_in, w_all, first, twist, second, second_back, first_back,
    rim, wide_k, wide_v, wide_q, turned_h, turned_x, mixed, queries,
    h_send, h_recv, x_send, x_recv, flat, spectra, y_flat, y_send, y_recv, back,
    gated, far_send, far_recv, near_send, near_recv,
    load_sem, rim_sems, w_load_sem, w_sems, h_sems, x_sems, y_sems, gated_sems, far_sems, near_sems,
):
    me_dp, me = lax.axis_index("dp"), lax.axis_index("ctx")
    chip, core = me_dp // 2, me_dp % 2
    pair = (chip * 2 + 1 - core, me)
    right = (lax.rem(chip + 1, CHIPS) * 2 + core, me)
    left = (lax.rem(chip + CHIPS - 1, CHIPS) * 2 + core, me)

    def partner(turn):
        step = PARTS - 2 - turn
        away = jnp.where(step % 2 == 0, step // 2 + 1, PARTS - (step + 1) // 2)
        return lax.rem(me + away, PARTS)

    barrier = pltpu.get_barrier_semaphore()

    @pl.loop(0, PARTS - 1)
    def _(step):
        pl.semaphore_signal(barrier, inc=1, device_id=(me_dp, partner(step)), device_id_type=MESH)

    for other in (pair, right, left):
        pl.semaphore_signal(barrier, inc=1, device_id=other, device_id_type=MESH)

    loads = [
        pltpu.make_async_copy(source, target, load_sem.at[n])
        for n, (source, target) in enumerate(
            [
                (h_hbm, h_in), (k_hbm, k_in), (v_hbm, v_in), (q_hbm, q_in),
                (first_hbm, first), (twist_hbm, twist), (second_hbm, second),
                (second_back_hbm, second_back), (first_back_hbm, first_back),
            ]
        )
    ]
    for load in loads:
        load.start()

    def remote(source, target, sems, n, device):
        return pltpu.make_async_remote_copy(
            src_ref=source, dst_ref=target, send_sem=sems.at[(0, *n)], recv_sem=sems.at[(1, *n)],
            device_id=device, device_id_type=MESH,
        )

    loads[0].wait()

    @pl.loop(0, CUTS)
    def _(cut):
        rows = pl.ds(pl.multiple_of(cut * SIDE, SIDE), SIDE)
        for tile in range(CHANNELS // SIDE):
            lanes = slice(tile * SIDE, (tile + 1) * SIDE)
            turned_h[cut, lanes, :] = h_in[rows, lanes].astype(F32).T

    def packed(turned, chunk, device):
        rows = pl.ds(pl.multiple_of(chunk * PARTS * CHUNK + device * CHUNK, CHUNK), CHUNK)
        return jnp.concatenate([turned[cut, rows, :] for cut in range(CUTS)], axis=0).astype(BF16)

    @pl.loop(0, PARTS)
    def _(device):
        for chunk in range(2):
            h_send[chunk, device] = packed(turned_h, chunk, device)

    for chunk in range(2):
        h_recv[chunk, me] = h_send[chunk, me]

    def widen(source, target):
        target[8 : 8 + ROWS, :] = source[...].astype(F32)

    def arrive(stream, target):
        target[0:8, :] = jnp.where(me > 0, rim[stream].astype(F32)[8:16, :], 0.0)

    def short(wide, stream, cut, lanes):
        window = wide[pl.ds(pl.multiple_of(cut * SIDE, SIDE), SIDE + 8), lanes]
        return (
            taps_ref[stream, 0:1, lanes] * window[8:]
            + taps_ref[stream, 1:2, lanes] * window[7:-1]
            + taps_ref[stream, 2:3, lanes] * window[6:-2]
        )

    def mix(first_cut, last_cut):
        @pl.loop(first_cut, last_cut)
        def _(cut):
            rows = pl.ds(pl.multiple_of(cut * SIDE, SIDE), SIDE)
            for tile in range(CHANNELS // SIDE):
                lanes = slice(tile * SIDE, (tile + 1) * SIDE)
                value = (short(wide_k, 1, cut, lanes) * short(wide_v, 2, cut, lanes)).astype(BF16)
                mixed[rows, lanes] = value
                turned_x[cut, lanes, :] = value.astype(F32).T

    def query(first_cut, last_cut):
        @pl.loop(first_cut, last_cut)
        def _(cut):
            rows = pl.ds(pl.multiple_of(cut * SIDE, SIDE), SIDE)
            for tile in range(CHANNELS // SIDE):
                lanes = slice(tile * SIDE, (tile + 1) * SIDE)
                queries[rows, lanes] = short(wide_q, 0, cut, lanes)

    for load, source, target in zip(loads[1:4], (k_in, v_in, q_in), (wide_k, wide_v, wide_q)):
        load.wait()
        widen(source, target)
    mix(1, CUTS)
    query(1, CUTS)

    pl.semaphore_wait(barrier, PARTS - 1 + 3)

    rims = [
        remote(hbm.at[pl.ds(ROWS - 16, 16)], rim.at[n], rim_sems, (n,), (me_dp, lax.rem(me + 1, PARTS)))
        for n, hbm in enumerate([q_hbm, k_hbm, v_hbm])
    ]
    for copy in rims:
        copy.start()

    def everyone(send, recv, sems, chunk):
        some = pl.ds(0, PARTS - 1)
        return remote(
            send.at[chunk, some], recv.at[chunk, some], sems, (chunk,), (me_dp, lax.rem(me + 1, PARTS))
        )

    def send_filter(chunk):
        @pl.loop(0, PARTS - 1)
        def _(step):
            to = partner(step)
            remote(h_send.at[chunk, to], h_recv.at[chunk, me], h_sems, (chunk,), (me_dp, to)).start()

        return everyone(h_send, h_recv, h_sems, chunk)

    def send_mixed(chunk):
        @pl.loop(0, PARTS - 1)
        def _(step):
            to = partner(step)
            x_send[chunk, to] = packed(turned_x, chunk, to)
            remote(x_send.at[chunk, to], x_recv.at[chunk, me], x_sems, (chunk,), (me_dp, to)).start()

        x_recv[chunk, me] = packed(turned_x, chunk, me)
        return everyone(x_send, x_recv, x_sems, chunk)

    h_all, x_all = {}, {}
    h_all[0] = send_filter(0)
    rims[1].wait()
    rims[2].wait()
    arrive(1, wide_k)
    arrive(2, wide_v)
    mix(0, 1)
    x_all[0] = send_mixed(0)

    def columns(chip_to, core_to):
        return pl.ds(pl.multiple_of((chip_to * 2 + core_to) * COLUMNS, COLUMNS), COLUMNS)

    w_loads = [
        pltpu.make_async_copy(w_hbm.at[:, columns(n, core)], w_all.at[core, n], w_load_sem.at[n])
        for n in range(CHIPS)
    ]
    w_sent = [
        remote(w_hbm.at[:, columns(n, 1 - core)], w_all.at[core, n], w_sems, (n,), pair)
        for n in range(CHIPS)
    ]
    for copy in w_loads + w_sent:
        copy.start()

    def spectrum(base):
        data = jnp.concatenate(
            [flat[pl.ds(base + n, SIDE, stride=CHUNK), :] for n in range(2)], axis=1
        ).astype(BF16)
        part = jnp.dot(first[...], jnp.concatenate([data, data], axis=0), preferred_element_type=F32)
        rows = []
        for n in range(2):
            lanes = slice(n * SIDE, (n + 1) * SIDE)
            real, imag = part[:SIDE, lanes], part[SIDE:, lanes]
            rows.append(
                jnp.concatenate(
                    [real * twist[0] - imag * twist[1], real * twist[1] + imag * twist[0]], axis=1
                )
            )
        high, low = split(jnp.concatenate(rows, axis=0))
        return jnp.dot(
            jnp.concatenate([high, low, high], axis=1), second[...], preferred_element_type=F32
        )

    def unpack(arrived, chunk):
        @pl.loop(0, PARTS)
        def _(source):
            rows = pl.ds(pl.multiple_of(source * CUTS * CHUNK, CUTS * CHUNK), CUTS * CHUNK)
            flat[rows, :] = arrived[chunk, source].astype(F32)

    def filter_spectra(chunk):
        h_all[chunk].wait_recv()
        unpack(h_recv, chunk)

        for step in range(CHUNK // 2):
            spectra[chunk * (CHUNK // 2) + step] = spectrum(step * 2)

    def convolve(chunk):
        x_all[chunk].wait_recv()
        unpack(x_recv, chunk)

        def invert(x_spec, step):
            h_spec = spectra[chunk * (CHUNK // 2) + step]
            x_real, x_imag = x_spec[:, :SIDE], x_spec[:, SIDE:]
            h_real, h_imag = h_spec[:, :SIDE], h_spec[:, SIDE:]
            high, low = split(
                jnp.concatenate(
                    [x_real * h_real - x_imag * h_imag, x_real * h_imag + x_imag * h_real], axis=1
                )
            )
            product = jnp.dot(
                jnp.concatenate([high, low, high], axis=1),
                second_back[...],
                preferred_element_type=F32,
            )
            stacked = []
            for n in range(2):
                rows = slice(n * SIDE, (n + 1) * SIDE)
                real, imag = product[rows, :SIDE], product[rows, SIDE:]
                high, low = split(
                    jnp.concatenate(
                        [real * twist[0] + imag * twist[1], imag * twist[0] - real * twist[1]], axis=0
                    )
                )
                stacked.append(jnp.concatenate([high, low, high], axis=0))
            values = jnp.dot(
                first_back[...], jnp.concatenate(stacked, axis=1), preferred_element_type=F32
            )
            for n in range(2):
                y_flat[pl.ds(step * 2 + n, SIDE, stride=CHUNK), :] = values[:, n * SIDE : (n + 1) * SIDE]

        x_spec = spectrum(0)
        for step in range(CHUNK // 2):
            later = spectrum(step * 2 + 2) if step + 1 < CHUNK // 2 else None
            invert(x_spec, step)
            x_spec = later

        @pl.loop(0, PARTS)
        def _(device):
            rows = pl.ds(pl.multiple_of(device * CUTS * CHUNK, CUTS * CHUNK), CUTS * CHUNK)
            value = y_flat[rows, :].astype(BF16)
            for half in range(2):
                y_send[chunk, half, device] = value[half * 16 : (half + 1) * 16]

    def send_back(chunk, half):
        @pl.loop(0, PARTS - 1)
        def _(step):
            to = partner(step)
            remote(
                y_send.at[chunk, half, to], y_recv.at[chunk, half, me], y_sems, (chunk, half),
                (me_dp, to),
            ).start()

        y_recv[chunk, half, me] = y_send[chunk, half, me]
        some = pl.ds(0, PARTS - 1)
        return remote(
            y_send.at[chunk, half, some], y_recv.at[chunk, half, some], y_sems, (chunk, half),
            (me_dp, lax.rem(me + 1, PARTS)),
        )

    for load in loads[4:]:
        load.wait()
    y_all = {}
    h_all[0].wait_send()
    h_all[1] = send_filter(1)
    filter_spectra(0)
    x_all[0].wait_send()
    x_all[1] = send_mixed(1)
    convolve(0)
    y_all[0, 0] = send_back(0, 0)
    filter_spectra(1)
    convolve(1)
    y_all[1, 0] = send_back(1, 0)

    def gate(chunk, half):
        y_all[chunk, half].wait_recv()

        @pl.loop(0, PARTS)
        def _(source):
            value = y_recv[chunk, half, source].astype(F32)
            rows = pl.ds(pl.multiple_of(source * CHUNK, CHUNK), CHUNK)
            for n in range(2):
                back[n, rows, :] = value[n * CHUNK : (n + 1) * CHUNK, :]

        @pl.loop(0, 2)
        def _(n):
            rows = pl.ds(pl.multiple_of(half * HALF + n * SIDE, SIDE), SIDE)
            for tile in range(PARTS * CHUNK // SIDE):
                first_lane = chunk * PARTS * CHUNK + tile * SIDE
                lanes = slice(first_lane, first_lane + SIDE)
                convolved = back[n, tile * SIDE : (tile + 1) * SIDE, :].T
                direct = skip_ref[0:1, lanes] * mixed[rows, lanes].astype(F32)
                gated[core, rows, lanes] = (queries[rows, lanes] * (convolved + direct)).astype(BF16)

        lanes = pl.ds(chunk * PARTS * CHUNK, PARTS * CHUNK)
        block = gated.at[core, pl.ds(half * HALF, HALF), lanes]
        copy = remote(block, block, gated_sems, (chunk, half), pair)
        copy.start()
        return copy

    def partial(half, to, strip):
        rows, lanes = slice(half * HALF, (half + 1) * HALF), slice(strip * STRIP, (strip + 1) * STRIP)
        return jnp.dot(
            gated[0, rows, :], w_all[0, to, :, lanes], preferred_element_type=F32
        ) + jnp.dot(gated[1, rows, :], w_all[1, to, :, lanes], preferred_element_type=F32)

    chip_right, chip_left = lax.rem(chip + 1, CHIPS), lax.rem(chip + CHIPS - 1, CHIPS)
    chip_across = lax.rem(chip + 2, CHIPS)
    far, near = {}, {}
    ways = ((0, right, chip_right), (1, left, chip_left))

    def send_far(half):
        for way, device, _ in ways:
            far_send[half, way] = partial(half, chip_across, way).astype(BF16)
            far[half, way] = remote(
                far_send.at[half, way], far_recv.at[half, way], far_sems, (half, way), device
            )
            far[half, way].start()

    def send_near(half, passed):
        for way, device, to in ways:
            strip = way if passed else 1 - way
            value = partial(half, to, strip)
            if passed:
                far[half, way].wait_recv()
                value = value + far_recv[half, way].astype(F32)
            near_send[half, way, strip] = value.astype(BF16)
            near[half, way, strip] = remote(
                near_send.at[half, way, strip], near_recv.at[half, way, strip], near_sems,
                (half, way, strip), device,
            )
            near[half, way, strip].start()

    def finish(half):
        for strip in range(2):
            value = partial(half, chip, strip)
            for way in range(2):
                near[half, way, strip].wait_recv()
                value = value + near_recv[half, way, strip].astype(F32)
            out_ref[half * HALF : (half + 1) * HALF, strip * STRIP : (strip + 1) * STRIP] = value.astype(BF16)

    rims[0].wait()
    arrive(0, wide_q)
    query(0, 1)
    exchanged = [gate(0, 0)]
    y_all[1, 0].wait_send()
    y_all[0, 1] = send_back(0, 1)
    y_all[1, 1] = send_back(1, 1)
    exchanged.append(gate(1, 0))
    for copy in w_loads + w_sent + exchanged:
        copy.wait()
    send_far(0)
    send_near(0, False)
    exchanged = [gate(0, 1), gate(1, 1)]
    for copy in exchanged:
        copy.wait()
    send_far(1)
    send_near(0, True)
    send_near(1, False)
    send_near(1, True)
    finish(0)
    finish(1)

    y_all[0, 0].wait_send()
    for copy in [h_all[1], x_all[1], y_all[0, 1], y_all[1, 1], *far.values(), *near.values()]:
        copy.wait_send()


def body(q_proj, k_proj, v_proj, short_taps, long_filter, skip_gain, w_out):
    constants = [jnp.asarray(t) for t in tables(SIDE)]
    wide = (8 + ROWS, CHANNELS)
    stream = (ROWS, CHANNELS)
    travel = (2, PARTS, CUTS * CHUNK, SIDE)
    pieces = (2, 2, PARTS, 16, SIDE)
    dma = pltpu.SemaphoreType.DMA
    anywhere = pl.BlockSpec(memory_space=pl.ANY)
    local = pl.BlockSpec(memory_space=pltpu.VMEM)
    return pl.pallas_call(
        kernel,
        out_shape=jax.ShapeDtypeStruct((ROWS, COLUMNS), BF16),
        in_specs=[anywhere] * 5 + [local] * 2 + [anywhere] * 5,
        out_specs=local,
        scratch_shapes=[
            *[pltpu.VMEM(stream, BF16)] * 4,
            pltpu.VMEM((2, CHIPS, CHANNELS, COLUMNS), BF16),
            *[pltpu.VMEM(t.shape, t.dtype) for t in constants],
            pltpu.VMEM((3, 16, CHANNELS), BF16),
            *[pltpu.VMEM(wide, F32)] * 3,
            *[pltpu.VMEM((CUTS, CHANNELS, SIDE), F32)] * 2,
            pltpu.VMEM(stream, BF16),
            pltpu.VMEM(stream, F32),
            *[pltpu.VMEM(travel, BF16)] * 4,
            pltpu.VMEM((SIDE * CHUNK, SIDE), F32),
            pltpu.VMEM((CHUNK, 2 * SIDE, 2 * SIDE), F32),
            pltpu.VMEM((SIDE * CHUNK, SIDE), F32),
            *[pltpu.VMEM(pieces, BF16)] * 2,
            pltpu.VMEM((2, PARTS * CHUNK, SIDE), F32),
            pltpu.VMEM((2, ROWS, CHANNELS), BF16),
            *[pltpu.VMEM((2, 2, HALF, STRIP), BF16)] * 2,
            *[pltpu.VMEM((2, 2, 2, HALF, STRIP), BF16)] * 2,
            dma((9,)),
            dma((2, 3)),
            dma((CHIPS,)),
            dma((2, CHIPS)),
            dma((2, 2)),
            dma((2, 2)),
            dma((2, 2, 2)),
            dma((2, 2, 2)),
            dma((2, 2, 2)),
            dma((2, 2, 2, 2)),
        ],
        compiler_params=pltpu.CompilerParams(
            collective_id=0, has_side_effects=True, vmem_limit_bytes=56 * 1024 * 1024
        ),
    )(
        q_proj, k_proj, v_proj, long_filter, w_out, short_taps, skip_gain[None, :], *constants
    )


def solution(mesh):
    placed = (
        P("ctx", "dp"),
        P("ctx", "dp"),
        P("ctx", "dp"),
        P(None, None, "dp"),
        P("ctx", "dp"),
        P("dp"),
        P("dp", None),
    )
    return jax.shard_map(
        body, mesh=mesh, in_specs=placed, out_specs=P("ctx", "dp"), check_vma=False
    )
```

```python
import functools
import math

import jax
import jax.numpy as jnp
import ml_dtypes
import numpy as np
from jax import lax
from jax.experimental import pallas as pl
from jax.experimental.pallas import tpu as pltpu
from jax.sharding import PartitionSpec as P

BF16 = jnp.bfloat16
F32 = jnp.float32
MESH = pl.DeviceIdType.MESH

ROWS = 512
CHANNELS = 512
PARTS = 32
CHIPS = 4
SIDE = 128
CUTS = ROWS // SIDE
CHUNK = 8
COLUMNS = 512
HALF = ROWS // 2
STRIP = COLUMNS // 2


def halves(table):
    high = table.astype(ml_dtypes.bfloat16)
    low = (table - high.astype(np.float64)).astype(ml_dtypes.bfloat16)
    return high, low


@functools.lru_cache(None)
def tables(side):
    total = side * side
    index = np.arange(side)
    quarter = index + 0.25
    outer = -2.0 * math.pi * quarter[:, None] * index[None, :] / side
    high, low = halves(np.concatenate([np.cos(outer), np.sin(outer)], axis=0))
    first = np.concatenate([high, low], axis=1)
    turn = -2.0 * math.pi * quarter[:, None] * index[None, :] / total
    twist = np.stack([np.cos(turn), np.sin(turn)]).astype(np.float32)
    inner = -2.0 * math.pi * index[:, None] * index[None, :] / side
    cosine, sine = np.cos(inner), np.sin(inner)
    high, low = halves(np.block([[cosine, sine], [-sine, cosine]]))
    second = np.concatenate([high, high, low], axis=0)
    high, low = halves(np.block([[cosine, -sine], [sine, cosine]]))
    second_back = np.concatenate([high, high, low], axis=0)
    high, low = halves(np.concatenate([np.cos(outer).T, np.sin(outer).T], axis=1) / total)
    first_back = np.concatenate([high, high, low], axis=1)
    return first, twist, second, second_back, first_back


def split(value):
    high = value.astype(BF16)
    low = (value - high.astype(F32)).astype(BF16)
    return high, low


def kernel(
    q_hbm, k_hbm, v_hbm, h_hbm, w_hbm, taps_ref, skip_ref,
    first_hbm, twist_hbm, second_hbm, second_back_hbm, first_back_hbm,
    out_hbm,
    q_in, k_in, v_in, h_in, w_all, first, twist, second, second_back, first_back,
    rim, wide_k, wide_v, wide_q, turned_h, turned_x, mixed, queries,
    h_send, h_recv, x_send, x_recv, flat, spectra, y_flat, y_send, y_recv, back,
    gated, far_send, far_recv, near_send, near_recv, result,
    load_sem, out_sem, rim_sems, w_load_sem, w_sems, h_sems, x_sems, y_sems, gated_sems, far_sems, near_sems,
):
    me_dp, me = lax.axis_index("dp"), lax.axis_index("ctx")
    chip, core = me_dp // 2, me_dp % 2
    pair = (chip * 2 + 1 - core, me)
    right = (lax.rem(chip + 1, CHIPS) * 2 + core, me)
    left = (lax.rem(chip + CHIPS - 1, CHIPS) * 2 + core, me)

    def partner(turn):
        step = PARTS - 2 - turn
        away = jnp.where(step % 2 == 0, step // 2 + 1, PARTS - (step + 1) // 2)
        return lax.rem(me + away, PARTS)

    barrier = pltpu.get_barrier_semaphore()

    @pl.loop(0, PARTS - 1)
    def _(step):
        pl.semaphore_signal(barrier, inc=1, device_id=(me_dp, partner(step)), device_id_type=MESH)

    for other in (pair, right, left):
        pl.semaphore_signal(barrier, inc=1, device_id=other, device_id_type=MESH)

    loads = [
        pltpu.make_async_copy(source, target, load_sem.at[n])
        for n, (source, target) in enumerate(
            [
                (h_hbm, h_in), (k_hbm, k_in), (v_hbm, v_in), (q_hbm, q_in),
                (first_hbm, first), (twist_hbm, twist), (second_hbm, second),
                (second_back_hbm, second_back), (first_back_hbm, first_back),
            ]
        )
    ]
    for load in loads:
        load.start()

    def remote(source, target, sems, n, device):
        return pltpu.make_async_remote_copy(
            src_ref=source, dst_ref=target, send_sem=sems.at[(0, *n)], recv_sem=sems.at[(1, *n)],
            device_id=device, device_id_type=MESH,
        )

    loads[0].wait()

    @pl.loop(0, CUTS)
    def _(cut):
        rows = pl.ds(pl.multiple_of(cut * SIDE, SIDE), SIDE)
        for tile in range(CHANNELS // SIDE):
            lanes = slice(tile * SIDE, (tile + 1) * SIDE)
            turned_h[cut, lanes, :] = h_in[rows, lanes].astype(F32).T

    def packed(turned, chunk, device):
        rows = pl.ds(pl.multiple_of(chunk * PARTS * CHUNK + device * CHUNK, CHUNK), CHUNK)
        return jnp.concatenate([turned[cut, rows, :] for cut in range(CUTS)], axis=0).astype(BF16)

    @pl.loop(0, PARTS)
    def _(device):
        for chunk in range(2):
            h_send[chunk, device] = packed(turned_h, chunk, device)

    for chunk in range(2):
        h_recv[chunk, me] = h_send[chunk, me]

    def widen(source, target):
        target[8 : 8 + ROWS, :] = source[...].astype(F32)

    def arrive(stream, target):
        target[0:8, :] = jnp.where(me > 0, rim[stream].astype(F32)[8:16, :], 0.0)

    def short(wide, stream, cut, lanes):
        window = wide[pl.ds(pl.multiple_of(cut * SIDE, SIDE), SIDE + 8), lanes]
        return (
            taps_ref[stream, 0:1, lanes] * window[8:]
            + taps_ref[stream, 1:2, lanes] * window[7:-1]
            + taps_ref[stream, 2:3, lanes] * window[6:-2]
        )

    def mix(first_cut, last_cut):
        @pl.loop(first_cut, last_cut)
        def _(cut):
            rows = pl.ds(pl.multiple_of(cut * SIDE, SIDE), SIDE)
            for tile in range(CHANNELS // SIDE):
                lanes = slice(tile * SIDE, (tile + 1) * SIDE)
                value = (short(wide_k, 1, cut, lanes) * short(wide_v, 2, cut, lanes)).astype(BF16)
                mixed[rows, lanes] = value
                turned_x[cut, lanes, :] = value.astype(F32).T

    def query(first_cut, last_cut):
        @pl.loop(first_cut, last_cut)
        def _(cut):
            rows = pl.ds(pl.multiple_of(cut * SIDE, SIDE), SIDE)
            for tile in range(CHANNELS // SIDE):
                lanes = slice(tile * SIDE, (tile + 1) * SIDE)
                queries[rows, lanes] = short(wide_q, 0, cut, lanes)

    for load, source, target in zip(loads[1:4], (k_in, v_in, q_in), (wide_k, wide_v, wide_q)):
        load.wait()
        widen(source, target)
    mix(1, CUTS)
    query(1, CUTS)

    pl.semaphore_wait(barrier, PARTS - 1 + 3)

    rims = [
        remote(hbm.at[pl.ds(ROWS - 16, 16)], rim.at[n], rim_sems, (n,), (me_dp, lax.rem(me + 1, PARTS)))
        for n, hbm in enumerate([q_hbm, k_hbm, v_hbm])
    ]
    for copy in rims:
        copy.start()

    def everyone(send, recv, sems, chunk):
        some = pl.ds(0, PARTS - 1)
        return remote(
            send.at[chunk, some], recv.at[chunk, some], sems, (chunk,), (me_dp, lax.rem(me + 1, PARTS))
        )

    def send_filter(chunk):
        @pl.loop(0, PARTS - 1)
        def _(step):
            to = partner(step)
            remote(h_send.at[chunk, to], h_recv.at[chunk, me], h_sems, (chunk,), (me_dp, to)).start()

        return everyone(h_send, h_recv, h_sems, chunk)

    def send_mixed(chunk):
        @pl.loop(0, PARTS - 1)
        def _(step):
            to = partner(step)
            x_send[chunk, to] = packed(turned_x, chunk, to)
            remote(x_send.at[chunk, to], x_recv.at[chunk, me], x_sems, (chunk,), (me_dp, to)).start()

        x_recv[chunk, me] = packed(turned_x, chunk, me)
        return everyone(x_send, x_recv, x_sems, chunk)

    h_all, x_all = {}, {}
    h_all[0] = send_filter(0)
    rims[1].wait()
    rims[2].wait()
    arrive(1, wide_k)
    arrive(2, wide_v)
    mix(0, 1)
    x_all[0] = send_mixed(0)

    def columns(chip_to, core_to):
        return pl.ds(pl.multiple_of((chip_to * 2 + core_to) * COLUMNS, COLUMNS), COLUMNS)

    w_loads = [
        pltpu.make_async_copy(w_hbm.at[:, columns(n, core)], w_all.at[core, n], w_load_sem.at[n])
        for n in range(CHIPS)
    ]
    w_sent = [
        remote(w_hbm.at[:, columns(n, 1 - core)], w_all.at[core, n], w_sems, (n,), pair)
        for n in range(CHIPS)
    ]
    for copy in w_loads + w_sent:
        copy.start()

    def spectrum(base):
        data = jnp.concatenate(
            [flat[pl.ds(base + n, SIDE, stride=CHUNK), :] for n in range(2)], axis=1
        ).astype(BF16)
        part = jnp.dot(first[...], jnp.concatenate([data, data], axis=0), preferred_element_type=F32)
        rows = []
        for n in range(2):
            lanes = slice(n * SIDE, (n + 1) * SIDE)
            real, imag = part[:SIDE, lanes], part[SIDE:, lanes]
            rows.append(
                jnp.concatenate(
                    [real * twist[0] - imag * twist[1], real * twist[1] + imag * twist[0]], axis=1
                )
            )
        high, low = split(jnp.concatenate(rows, axis=0))
        return jnp.dot(
            jnp.concatenate([high, low, high], axis=1), second[...], preferred_element_type=F32
        )

    def unpack(arrived, chunk):
        @pl.loop(0, PARTS)
        def _(source):
            rows = pl.ds(pl.multiple_of(source * CUTS * CHUNK, CUTS * CHUNK), CUTS * CHUNK)
            flat[rows, :] = arrived[chunk, source].astype(F32)

    def filter_spectra(chunk):
        h_all[chunk].wait_recv()
        unpack(h_recv, chunk)

        for step in range(CHUNK // 2):
            spectra[chunk * (CHUNK // 2) + step] = spectrum(step * 2)

    def convolve(chunk):
        x_all[chunk].wait_recv()
        unpack(x_recv, chunk)

        def invert(x_spec, step):
            h_spec = spectra[chunk * (CHUNK // 2) + step]
            x_real, x_imag = x_spec[:, :SIDE], x_spec[:, SIDE:]
            h_real, h_imag = h_spec[:, :SIDE], h_spec[:, SIDE:]
            high, low = split(
                jnp.concatenate(
                    [x_real * h_real - x_imag * h_imag, x_real * h_imag + x_imag * h_real], axis=1
                )
            )
            product = jnp.dot(
                jnp.concatenate([high, low, high], axis=1),
                second_back[...],
                preferred_element_type=F32,
            )
            stacked = []
            for n in range(2):
                rows = slice(n * SIDE, (n + 1) * SIDE)
                real, imag = product[rows, :SIDE], product[rows, SIDE:]
                high, low = split(
                    jnp.concatenate(
                        [real * twist[0] + imag * twist[1], imag * twist[0] - real * twist[1]], axis=0
                    )
                )
                stacked.append(jnp.concatenate([high, low, high], axis=0))
            values = jnp.dot(
                first_back[...], jnp.concatenate(stacked, axis=1), preferred_element_type=F32
            )
            for n in range(2):
                y_flat[pl.ds(step * 2 + n, SIDE, stride=CHUNK), :] = values[:, n * SIDE : (n + 1) * SIDE]

        x_spec = spectrum(0)
        for step in range(CHUNK // 2):
            later = spectrum(step * 2 + 2) if step + 1 < CHUNK // 2 else None
            invert(x_spec, step)
            x_spec = later

    def piece(device, half):
        rows = pl.ds(pl.multiple_of(device * CUTS * CHUNK + half * 16, 16), 16)
        return y_flat[rows, :].astype(BF16)

    def keep(chunk, half):
        @pl.loop(0, PARTS)
        def _(device):
            y_send[chunk, half, device] = piece(device, half)

    def send_back(chunk, half):
        @pl.loop(0, PARTS - 1)
        def _(step):
            to = partner(step)
            if half == 0:
                y_send[chunk, half, to] = piece(to, half)
            remote(
                y_send.at[chunk, half, to], y_recv.at[chunk, half, me], y_sems, (chunk, half),
                (me_dp, to),
            ).start()

        y_recv[chunk, half, me] = y_send[chunk, half, me] if half else piece(me, half)
        some = pl.ds(0, PARTS - 1)
        return remote(
            y_send.at[chunk, half, some], y_recv.at[chunk, half, some], y_sems, (chunk, half),
            (me_dp, lax.rem(me + 1, PARTS)),
        )

    for load in loads[4:]:
        load.wait()
    y_all = {}
    h_all[0].wait_send()
    h_all[1] = send_filter(1)
    filter_spectra(0)
    x_all[0].wait_send()
    x_all[1] = send_mixed(1)
    convolve(0)
    y_all[0, 0] = send_back(0, 0)
    keep(0, 1)
    filter_spectra(1)
    convolve(1)
    y_all[1, 0] = send_back(1, 0)
    keep(1, 1)

    def gate(chunk, half):
        y_all[chunk, half].wait_recv()

        @pl.loop(0, PARTS)
        def _(source):
            value = y_recv[chunk, half, source].astype(F32)
            rows = pl.ds(pl.multiple_of(source * CHUNK, CHUNK), CHUNK)
            for n in range(2):
                back[n, rows, :] = value[n * CHUNK : (n + 1) * CHUNK, :]

        @pl.loop(0, 2)
        def _(n):
            rows = pl.ds(pl.multiple_of(half * HALF + n * SIDE, SIDE), SIDE)
            for tile in range(PARTS * CHUNK // SIDE):
                first_lane = chunk * PARTS * CHUNK + tile * SIDE
                lanes = slice(first_lane, first_lane + SIDE)
                convolved = back[n, tile * SIDE : (tile + 1) * SIDE, :].T
                direct = skip_ref[0:1, lanes] * mixed[rows, lanes].astype(F32)
                gated[core, rows, lanes] = (queries[rows, lanes] * (convolved + direct)).astype(BF16)

        lanes = pl.ds(chunk * PARTS * CHUNK, PARTS * CHUNK)
        block = gated.at[core, pl.ds(half * HALF, HALF), lanes]
        copy = remote(block, block, gated_sems, (chunk, half), pair)
        copy.start()
        return copy

    def partial(half, to, strip):
        rows, lanes = slice(half * HALF, (half + 1) * HALF), slice(strip * STRIP, (strip + 1) * STRIP)
        return jnp.dot(
            gated[0, rows, :], w_all[0, to, :, lanes], preferred_element_type=F32
        ) + jnp.dot(gated[1, rows, :], w_all[1, to, :, lanes], preferred_element_type=F32)

    chip_right, chip_left = lax.rem(chip + 1, CHIPS), lax.rem(chip + CHIPS - 1, CHIPS)
    chip_across = lax.rem(chip + 2, CHIPS)
    far, near = {}, {}
    ways = ((0, right, chip_right), (1, left, chip_left))

    def send_far(half):
        for way, device, _ in ways:
            far_send[half, way] = partial(half, chip_across, way).astype(BF16)
            far[half, way] = remote(
                far_send.at[half, way], far_recv.at[half, way], far_sems, (half, way), device
            )
            far[half, way].start()

    def send_near(half, passed):
        for way, device, to in ways:
            strip = way if passed else 1 - way
            value = partial(half, to, strip)
            if passed:
                far[half, way].wait_recv()
                value = value + far_recv[half, way].astype(F32)
            near_send[half, way, strip] = value.astype(BF16)
            near[half, way, strip] = remote(
                near_send.at[half, way, strip], near_recv.at[half, way, strip], near_sems,
                (half, way, strip), device,
            )
            near[half, way, strip].start()

    def finish(half):
        for strip in range(2):
            value = partial(half, chip, strip)
            for way in range(2):
                near[half, way, strip].wait_recv()
                value = value + near_recv[half, way, strip].astype(F32)
            result[half, :, strip * STRIP : (strip + 1) * STRIP] = value.astype(BF16)
        copy = pltpu.make_async_copy(
            result.at[half], out_hbm.at[pl.ds(half * HALF, HALF)], out_sem.at[half]
        )
        copy.start()
        return copy

    rims[0].wait()
    arrive(0, wide_q)
    query(0, 1)
    exchanged = [gate(0, 0)]
    y_all[1, 0].wait_send()
    y_all[0, 1] = send_back(0, 1)
    y_all[1, 1] = send_back(1, 1)
    exchanged.append(gate(1, 0))
    for copy in w_loads + w_sent + exchanged:
        copy.wait()
    send_far(0)
    send_near(0, False)
    exchanged = [gate(0, 1), gate(1, 1)]
    for copy in exchanged:
        copy.wait()
    send_far(1)
    send_near(0, True)
    send_near(1, False)
    send_near(1, True)
    stored = [finish(0), finish(1)]

    for copy in stored:
        copy.wait()
    y_all[0, 0].wait_send()
    for copy in [h_all[1], x_all[1], y_all[0, 1], y_all[1, 1], *far.values(), *near.values()]:
        copy.wait_send()


def body(q_proj, k_proj, v_proj, short_taps, long_filter, skip_gain, w_out):
    constants = [jnp.asarray(t) for t in tables(SIDE)]
    wide = (8 + ROWS, CHANNELS)
    stream = (ROWS, CHANNELS)
    travel = (2, PARTS, CUTS * CHUNK, SIDE)
    pieces = (2, 2, PARTS, 16, SIDE)
    dma = pltpu.SemaphoreType.DMA
    anywhere = pl.BlockSpec(memory_space=pl.ANY)
    local = pl.BlockSpec(memory_space=pltpu.VMEM)
    return pl.pallas_call(
        kernel,
        out_shape=jax.ShapeDtypeStruct((ROWS, COLUMNS), BF16),
        in_specs=[anywhere] * 5 + [local] * 2 + [anywhere] * 5,
        out_specs=anywhere,
        scratch_shapes=[
            *[pltpu.VMEM(stream, BF16)] * 4,
            pltpu.VMEM((2, CHIPS, CHANNELS, COLUMNS), BF16),
            *[pltpu.VMEM(t.shape, t.dtype) for t in constants],
            pltpu.VMEM((3, 16, CHANNELS), BF16),
            *[pltpu.VMEM(wide, F32)] * 3,
            *[pltpu.VMEM((CUTS, CHANNELS, SIDE), F32)] * 2,
            pltpu.VMEM(stream, BF16),
            pltpu.VMEM(stream, F32),
            *[pltpu.VMEM(travel, BF16)] * 4,
            pltpu.VMEM((SIDE * CHUNK, SIDE), F32),
            pltpu.VMEM((CHUNK, 2 * SIDE, 2 * SIDE), F32),
            pltpu.VMEM((SIDE * CHUNK, SIDE), F32),
            *[pltpu.VMEM(pieces, BF16)] * 2,
            pltpu.VMEM((2, PARTS * CHUNK, SIDE), F32),
            pltpu.VMEM((2, ROWS, CHANNELS), BF16),
            *[pltpu.VMEM((2, 2, HALF, STRIP), BF16)] * 2,
            *[pltpu.VMEM((2, 2, 2, HALF, STRIP), BF16)] * 2,
            pltpu.VMEM((2, HALF, COLUMNS), BF16),
            dma((9,)),
            dma((2,)),
            dma((2, 3)),
            dma((CHIPS,)),
            dma((2, CHIPS)),
            dma((2, 2)),
            dma((2, 2)),
            dma((2, 2, 2)),
            dma((2, 2, 2)),
            dma((2, 2, 2)),
            dma((2, 2, 2, 2)),
        ],
        compiler_params=pltpu.CompilerParams(
            collective_id=0, has_side_effects=True, vmem_limit_bytes=56 * 1024 * 1024
        ),
    )(
        q_proj, k_proj, v_proj, long_filter, w_out, short_taps, skip_gain[None, :], *constants
    )


def solution(mesh):
    placed = (
        P("ctx", "dp"),
        P("ctx", "dp"),
        P("ctx", "dp"),
        P(None, None, "dp"),
        P("ctx", "dp"),
        P("dp"),
        P("dp", None),
    )
    return jax.shard_map(
        body, mesh=mesh, in_specs=placed, out_specs=P("ctx", "dp"), check_vma=False
    )
```

```python
import functools
import math

import jax
import jax.numpy as jnp
import ml_dtypes
import numpy as np
from jax import lax
from jax.experimental import pallas as pl
from jax.experimental.pallas import tpu as pltpu
from jax.sharding import PartitionSpec as P

BF16 = jnp.bfloat16
F32 = jnp.float32
MESH = pl.DeviceIdType.MESH

ROWS = 512
CHANNELS = 512
PARTS = 32
CHIPS = 4
SIDE = 128
CUTS = ROWS // SIDE
CHUNK = 8
COLUMNS = 512
HALF = ROWS // 2
STRIP = COLUMNS // 2


def halves(table):
    high = table.astype(ml_dtypes.bfloat16)
    low = (table - high.astype(np.float64)).astype(ml_dtypes.bfloat16)
    return high, low


@functools.lru_cache(None)
def tables(side):
    total = side * side
    index = np.arange(side)
    quarter = index + 0.25
    outer = -2.0 * math.pi * quarter[:, None] * index[None, :] / side
    high, low = halves(np.concatenate([np.cos(outer), np.sin(outer)], axis=0))
    first = np.concatenate([high, low], axis=1)
    turn = -2.0 * math.pi * quarter[:, None] * index[None, :] / total
    twist = np.stack([np.cos(turn), np.sin(turn)]).astype(np.float32)
    inner = -2.0 * math.pi * index[:, None] * index[None, :] / side
    cosine, sine = np.cos(inner), np.sin(inner)
    high, low = halves(np.block([[cosine, sine], [-sine, cosine]]))
    second = np.concatenate([high, high, low], axis=0)
    high, low = halves(np.block([[cosine, -sine], [sine, cosine]]))
    second_back = np.concatenate([high, high, low], axis=0)
    high, low = halves(np.concatenate([np.cos(outer).T, np.sin(outer).T], axis=1) / total)
    first_back = np.concatenate([high, high, low], axis=1)
    return first, twist, second, second_back, first_back


def split(value):
    high = value.astype(BF16)
    low = (value - high.astype(F32)).astype(BF16)
    return high, low


def kernel(
    q_hbm, k_hbm, v_hbm, h_hbm, w_hbm, taps_ref, skip_ref,
    first_hbm, twist_hbm, second_hbm, second_back_hbm, first_back_hbm,
    out_hbm,
    q_in, k_in, v_in, h_in, w_all, first, twist, second, second_back, first_back,
    rim, wide_k, wide_v, wide_q, turned_h, turned_x, mixed, queries,
    h_send, h_recv, x_send, x_recv, flat, spectra, y_flat, y_send, y_recv, back,
    gated, far_send, far_recv, near_send, near_recv, result,
    load_sem, out_sem, rim_sems, w_load_sem, w_sems, h_sems, x_sems, y_sems, gated_sems, far_sems, near_sems,
):
    me_dp, me = lax.axis_index("dp"), lax.axis_index("ctx")
    chip, core = me_dp // 2, me_dp % 2
    pair = (chip * 2 + 1 - core, me)
    right = (lax.rem(chip + 1, CHIPS) * 2 + core, me)
    left = (lax.rem(chip + CHIPS - 1, CHIPS) * 2 + core, me)

    def partner(turn):
        step = PARTS - 2 - turn
        away = jnp.where(step % 2 == 0, step // 2 + 1, PARTS - (step + 1) // 2)
        return lax.rem(me + away, PARTS)

    barrier = pltpu.get_barrier_semaphore()

    @pl.loop(0, PARTS - 1)
    def _(step):
        pl.semaphore_signal(barrier, inc=1, device_id=(me_dp, partner(step)), device_id_type=MESH)

    for other in (pair, right, left):
        pl.semaphore_signal(barrier, inc=1, device_id=other, device_id_type=MESH)

    loads = [
        pltpu.make_async_copy(source, target, load_sem.at[n])
        for n, (source, target) in enumerate(
            [
                (h_hbm, h_in), (k_hbm, k_in), (v_hbm, v_in), (q_hbm, q_in),
                (first_hbm, first), (twist_hbm, twist), (second_hbm, second),
                (second_back_hbm, second_back), (first_back_hbm, first_back),
            ]
        )
    ]
    for load in loads:
        load.start()

    def remote(source, target, sems, n, device):
        return pltpu.make_async_remote_copy(
            src_ref=source, dst_ref=target, send_sem=sems.at[(0, *n)], recv_sem=sems.at[(1, *n)],
            device_id=device, device_id_type=MESH,
        )

    loads[0].wait()

    @pl.loop(0, CUTS)
    def _(cut):
        rows = pl.ds(pl.multiple_of(cut * SIDE, SIDE), SIDE)
        for tile in range(CHANNELS // SIDE):
            lanes = slice(tile * SIDE, (tile + 1) * SIDE)
            turned_h[cut, lanes, :] = h_in[rows, lanes].astype(F32).T

    def packed(turned, chunk, device):
        rows = pl.ds(pl.multiple_of(chunk * PARTS * CHUNK + device * CHUNK, CHUNK), CHUNK)
        return jnp.concatenate([turned[cut, rows, :] for cut in range(CUTS)], axis=0).astype(BF16)

    @pl.loop(0, PARTS)
    def _(device):
        for chunk in range(2):
            h_send[chunk, device] = packed(turned_h, chunk, device)

    for chunk in range(2):
        h_recv[chunk, me] = h_send[chunk, me]

    def widen(source, target):
        target[8 : 8 + ROWS, :] = source[...].astype(F32)

    def arrive(stream, target):
        target[0:8, :] = jnp.where(me > 0, rim[stream].astype(F32)[8:16, :], 0.0)

    def short(wide, stream, cut, lanes):
        window = wide[pl.ds(pl.multiple_of(cut * SIDE, SIDE), SIDE + 8), lanes]
        return (
            taps_ref[stream, 0:1, lanes] * window[8:]
            + taps_ref[stream, 1:2, lanes] * window[7:-1]
            + taps_ref[stream, 2:3, lanes] * window[6:-2]
        )

    def mix(first_cut, last_cut):
        @pl.loop(first_cut, last_cut)
        def _(cut):
            rows = pl.ds(pl.multiple_of(cut * SIDE, SIDE), SIDE)
            for tile in range(CHANNELS // SIDE):
                lanes = slice(tile * SIDE, (tile + 1) * SIDE)
                value = (short(wide_k, 1, cut, lanes) * short(wide_v, 2, cut, lanes)).astype(BF16)
                mixed[rows, lanes] = value
                turned_x[cut, lanes, :] = value.astype(F32).T

    def query(first_cut, last_cut):
        @pl.loop(first_cut, last_cut)
        def _(cut):
            rows = pl.ds(pl.multiple_of(cut * SIDE, SIDE), SIDE)
            for tile in range(CHANNELS // SIDE):
                lanes = slice(tile * SIDE, (tile + 1) * SIDE)
                queries[rows, lanes] = short(wide_q, 0, cut, lanes)

    for load, source, target in zip(loads[1:4], (k_in, v_in, q_in), (wide_k, wide_v, wide_q)):
        load.wait()
        widen(source, target)
    mix(1, CUTS)
    query(1, CUTS)

    pl.semaphore_wait(barrier, PARTS - 1 + 3)

    rims = [
        remote(hbm.at[pl.ds(ROWS - 16, 16)], rim.at[n], rim_sems, (n,), (me_dp, lax.rem(me + 1, PARTS)))
        for n, hbm in enumerate([q_hbm, k_hbm, v_hbm])
    ]
    for copy in rims:
        copy.start()

    def everyone(send, recv, sems, chunk):
        some = pl.ds(0, PARTS - 1)
        return remote(
            send.at[chunk, some], recv.at[chunk, some], sems, (chunk,), (me_dp, lax.rem(me + 1, PARTS))
        )

    def send_filter(chunk):
        @pl.loop(0, PARTS - 1)
        def _(step):
            to = partner(step)
            remote(h_send.at[chunk, to], h_recv.at[chunk, me], h_sems, (chunk,), (me_dp, to)).start()

        return everyone(h_send, h_recv, h_sems, chunk)

    def send_mixed(chunk):
        @pl.loop(0, PARTS - 1)
        def _(step):
            to = partner(step)
            x_send[chunk, to] = packed(turned_x, chunk, to)
            remote(x_send.at[chunk, to], x_recv.at[chunk, me], x_sems, (chunk,), (me_dp, to)).start()

        x_recv[chunk, me] = packed(turned_x, chunk, me)
        return everyone(x_send, x_recv, x_sems, chunk)

    h_all, x_all = {}, {}
    h_all[0] = send_filter(0)
    rims[1].wait()
    rims[2].wait()
    arrive(1, wide_k)
    arrive(2, wide_v)
    mix(0, 1)
    x_all[0] = send_mixed(0)

    def columns(chip_to, core_to):
        return pl.ds(pl.multiple_of((chip_to * 2 + core_to) * COLUMNS, COLUMNS), COLUMNS)

    w_loads = [
        pltpu.make_async_copy(w_hbm.at[:, columns(n, core)], w_all.at[core, n], w_load_sem.at[n])
        for n in range(CHIPS)
    ]
    w_sent = [
        remote(w_hbm.at[:, columns(n, 1 - core)], w_all.at[core, n], w_sems, (n,), pair)
        for n in range(CHIPS)
    ]
    for copy in w_loads + w_sent:
        copy.start()

    def spectrum(base):
        data = jnp.concatenate(
            [flat[pl.ds(base + n, SIDE, stride=CHUNK), :] for n in range(2)], axis=1
        ).astype(BF16)
        part = jnp.dot(first[...], jnp.concatenate([data, data], axis=0), preferred_element_type=F32)
        rows = []
        for n in range(2):
            lanes = slice(n * SIDE, (n + 1) * SIDE)
            real, imag = part[:SIDE, lanes], part[SIDE:, lanes]
            rows.append(
                jnp.concatenate(
                    [real * twist[0] - imag * twist[1], real * twist[1] + imag * twist[0]], axis=1
                )
            )
        high, low = split(jnp.concatenate(rows, axis=0))
        return jnp.dot(
            jnp.concatenate([high, low, high], axis=1), second[...], preferred_element_type=F32
        )

    def unpack(arrived, chunk):
        @pl.loop(0, PARTS)
        def _(source):
            rows = pl.ds(pl.multiple_of(source * CUTS * CHUNK, CUTS * CHUNK), CUTS * CHUNK)
            flat[rows, :] = arrived[chunk, source].astype(F32)

    def filter_spectra(chunk):
        h_all[chunk].wait_recv()
        unpack(h_recv, chunk)

        for step in range(CHUNK // 2):
            spectra[chunk * (CHUNK // 2) + step] = spectrum(step * 2)

    def convolve(chunk):
        x_all[chunk].wait_recv()
        unpack(x_recv, chunk)

        def invert(x_spec, step):
            h_spec = spectra[chunk * (CHUNK // 2) + step]
            x_real, x_imag = x_spec[:, :SIDE], x_spec[:, SIDE:]
            h_real, h_imag = h_spec[:, :SIDE], h_spec[:, SIDE:]
            high, low = split(
                jnp.concatenate(
                    [x_real * h_real - x_imag * h_imag, x_real * h_imag + x_imag * h_real], axis=1
                )
            )
            product = jnp.dot(
                jnp.concatenate([high, low, high], axis=1),
                second_back[...],
                preferred_element_type=F32,
            )
            stacked = []
            for n in range(2):
                rows = slice(n * SIDE, (n + 1) * SIDE)
                real, imag = product[rows, :SIDE], product[rows, SIDE:]
                high, low = split(
                    jnp.concatenate(
                        [real * twist[0] + imag * twist[1], imag * twist[0] - real * twist[1]], axis=0
                    )
                )
                stacked.append(jnp.concatenate([high, low, high], axis=0))
            values = jnp.dot(
                first_back[...], jnp.concatenate(stacked, axis=1), preferred_element_type=F32
            )
            for n in range(2):
                y_flat[pl.ds(step * 2 + n, SIDE, stride=CHUNK), :] = values[:, n * SIDE : (n + 1) * SIDE]

        x_spec = spectrum(0)
        for step in range(CHUNK // 2):
            later = spectrum(step * 2 + 2) if step + 1 < CHUNK // 2 else None
            invert(x_spec, step)
            x_spec = later

    def piece(device, half):
        rows = pl.ds(pl.multiple_of(device * CUTS * CHUNK + half * 16, 16), 16)
        return y_flat[rows, :].astype(BF16)

    def keep(chunk, half):
        @pl.loop(0, PARTS)
        def _(device):
            y_send[chunk, half, device] = piece(device, half)

    def send_back(chunk, half):
        @pl.loop(0, PARTS - 1)
        def _(step):
            to = partner(step)
            if half == 0:
                y_send[chunk, half, to] = piece(to, half)
            remote(
                y_send.at[chunk, half, to], y_recv.at[chunk, half, me], y_sems, (chunk, half),
                (me_dp, to),
            ).start()

        y_recv[chunk, half, me] = y_send[chunk, half, me] if half else piece(me, half)
        some = pl.ds(0, PARTS - 1)
        return remote(
            y_send.at[chunk, half, some], y_recv.at[chunk, half, some], y_sems, (chunk, half),
            (me_dp, lax.rem(me + 1, PARTS)),
        )

    for load in loads[4:]:
        load.wait()
    y_all = {}
    h_all[0].wait_send()
    h_all[1] = send_filter(1)
    filter_spectra(0)
    x_all[0].wait_send()
    x_all[1] = send_mixed(1)
    convolve(0)
    y_all[0, 0] = send_back(0, 0)
    keep(0, 1)
    filter_spectra(1)
    convolve(1)
    y_all[1, 0] = send_back(1, 0)
    keep(1, 1)

    def gate(chunk, half):
        y_all[chunk, half].wait_recv()

        @pl.loop(0, PARTS)
        def _(source):
            value = y_recv[chunk, half, source].astype(F32)
            rows = pl.ds(pl.multiple_of(source * CHUNK, CHUNK), CHUNK)
            for n in range(2):
                back[n, rows, :] = value[n * CHUNK : (n + 1) * CHUNK, :]

        @pl.loop(0, 2)
        def _(n):
            rows = pl.ds(pl.multiple_of(half * HALF + n * SIDE, SIDE), SIDE)
            for tile in range(PARTS * CHUNK // SIDE):
                first_lane = chunk * PARTS * CHUNK + tile * SIDE
                lanes = slice(first_lane, first_lane + SIDE)
                convolved = back[n, tile * SIDE : (tile + 1) * SIDE, :].T
                direct = skip_ref[0:1, lanes] * mixed[rows, lanes].astype(F32)
                gated[core, rows, lanes] = (queries[rows, lanes] * (convolved + direct)).astype(BF16)

        lanes = pl.ds(chunk * PARTS * CHUNK, PARTS * CHUNK)
        block = gated.at[core, pl.ds(half * HALF, HALF), lanes]
        copy = remote(block, block, gated_sems, (chunk, half), pair)
        copy.start()
        return copy

    def partial(half, to, strip):
        rows, lanes = slice(half * HALF, (half + 1) * HALF), slice(strip * STRIP, (strip + 1) * STRIP)
        return jnp.dot(
            gated[0, rows, :], w_all[0, to, :, lanes], preferred_element_type=F32
        ) + jnp.dot(gated[1, rows, :], w_all[1, to, :, lanes], preferred_element_type=F32)

    chip_right, chip_left = lax.rem(chip + 1, CHIPS), lax.rem(chip + CHIPS - 1, CHIPS)
    chip_across = lax.rem(chip + 2, CHIPS)
    far, near = {}, {}
    ways = ((0, right, chip_right), (1, left, chip_left))

    def send_far(half):
        for way, device, _ in ways:
            far_send[half, way] = partial(half, chip_across, way).astype(BF16)
            far[half, way] = remote(
                far_send.at[half, way], far_recv.at[half, way], far_sems, (half, way), device
            )
            far[half, way].start()

    def send_near(half, passed):
        for way, device, to in ways:
            strip = way if passed else 1 - way
            value = partial(half, to, strip)
            if passed:
                far[half, way].wait_recv()
                value = value + far_recv[half, way].astype(F32)
            near_send[half, way, strip] = value.astype(BF16)
            near[half, way, strip] = remote(
                near_send.at[half, way, strip], near_recv.at[half, way, strip], near_sems,
                (half, way, strip), device,
            )
            near[half, way, strip].start()

    def finish(half):
        for strip in range(2):
            value = partial(half, chip, strip)
            for way in range(2):
                near[half, way, strip].wait_recv()
                value = value + near_recv[half, way, strip].astype(F32)
            result[half, :, strip * STRIP : (strip + 1) * STRIP] = value.astype(BF16)
        copy = pltpu.make_async_copy(
            result.at[half], out_hbm.at[pl.ds(half * HALF, HALF)], out_sem.at[half]
        )
        copy.start()
        return copy

    rims[0].wait()
    arrive(0, wide_q)
    query(0, 1)
    exchanged = [gate(0, 0)]
    y_all[1, 0].wait_send()
    y_all[0, 1] = send_back(0, 1)
    exchanged.append(gate(1, 0))
    y_all[1, 1] = send_back(1, 1)
    for copy in w_loads + w_sent + exchanged:
        copy.wait()
    send_far(0)
    send_near(0, False)
    exchanged = [gate(0, 1), gate(1, 1)]
    for copy in exchanged:
        copy.wait()
    send_far(1)
    send_near(0, True)
    send_near(1, False)
    send_near(1, True)
    stored = [finish(0), finish(1)]

    for copy in stored:
        copy.wait()
    y_all[0, 0].wait_send()
    for copy in [h_all[1], x_all[1], y_all[0, 1], y_all[1, 1], *far.values(), *near.values()]:
        copy.wait_send()


def body(q_proj, k_proj, v_proj, short_taps, long_filter, skip_gain, w_out):
    constants = [jnp.asarray(t) for t in tables(SIDE)]
    wide = (8 + ROWS, CHANNELS)
    stream = (ROWS, CHANNELS)
    travel = (2, PARTS, CUTS * CHUNK, SIDE)
    pieces = (2, 2, PARTS, 16, SIDE)
    dma = pltpu.SemaphoreType.DMA
    anywhere = pl.BlockSpec(memory_space=pl.ANY)
    local = pl.BlockSpec(memory_space=pltpu.VMEM)
    return pl.pallas_call(
        kernel,
        out_shape=jax.ShapeDtypeStruct((ROWS, COLUMNS), BF16),
        in_specs=[anywhere] * 5 + [local] * 2 + [anywhere] * 5,
        out_specs=anywhere,
        scratch_shapes=[
            *[pltpu.VMEM(stream, BF16)] * 4,
            pltpu.VMEM((2, CHIPS, CHANNELS, COLUMNS), BF16),
            *[pltpu.VMEM(t.shape, t.dtype) for t in constants],
            pltpu.VMEM((3, 16, CHANNELS), BF16),
            *[pltpu.VMEM(wide, F32)] * 3,
            *[pltpu.VMEM((CUTS, CHANNELS, SIDE), F32)] * 2,
            pltpu.VMEM(stream, BF16),
            pltpu.VMEM(stream, F32),
            *[pltpu.VMEM(travel, BF16)] * 4,
            pltpu.VMEM((SIDE * CHUNK, SIDE), F32),
            pltpu.VMEM((CHUNK, 2 * SIDE, 2 * SIDE), F32),
            pltpu.VMEM((SIDE * CHUNK, SIDE), F32),
            *[pltpu.VMEM(pieces, BF16)] * 2,
            pltpu.VMEM((2, PARTS * CHUNK, SIDE), F32),
            pltpu.VMEM((2, ROWS, CHANNELS), BF16),
            *[pltpu.VMEM((2, 2, HALF, STRIP), BF16)] * 2,
            *[pltpu.VMEM((2, 2, 2, HALF, STRIP), BF16)] * 2,
            pltpu.VMEM((2, HALF, COLUMNS), BF16),
            dma((9,)),
            dma((2,)),
            dma((2, 3)),
            dma((CHIPS,)),
            dma((2, CHIPS)),
            dma((2, 2)),
            dma((2, 2)),
            dma((2, 2, 2)),
            dma((2, 2, 2)),
            dma((2, 2, 2)),
            dma((2, 2, 2, 2)),
        ],
        compiler_params=pltpu.CompilerParams(
            collective_id=0, has_side_effects=True, vmem_limit_bytes=56 * 1024 * 1024
        ),
    )(
        q_proj, k_proj, v_proj, long_filter, w_out, short_taps, skip_gain[None, :], *constants
    )


def solution(mesh):
    placed = (
        P("ctx", "dp"),
        P("ctx", "dp"),
        P("ctx", "dp"),
        P(None, None, "dp"),
        P("ctx", "dp"),
        P("dp"),
        P("dp", None),
    )
    return jax.shard_map(
        body, mesh=mesh, in_specs=placed, out_specs=P("ctx", "dp"), check_vma=False
    )
```
